32 devices in a mesh: case: 4 (over y, x), tile: 8 (over z, core).
Axes of the slice: x: 2, y: 2, z: 4, core: 2. Of those that a mesh axis runs over, the one named last changes fastest.
Arguments:
- forcing: bfloat16 [4, 128, 512, 128], P('case', 'tile'), may hold values from -6 to 6
- permeability: float32 [4, 128, 512], P('case', 'tile'), may hold values from 0.05 to 1
- merge_weights: int32 [4], P('case'), may hold values from 4 to 6
- start_codes: int32 [2, 256, 128], replicated, may hold values from -7 to 7
Outputs:
- basis: bfloat16 [4, 65536, 128], P('case', 'tile')
The draws below stay inside these ranges and needn't reach their ends.
All inputs are finite; a program needn't handle non-finite values.
Results may differ from the reference program's by a relative error of at most 0.018.
Values may be sent and summed in bfloat16 or wider, within the bound.
A program may use at most 64 MiB of HBM per device.

```python
import math
import jax
import jax.numpy as jnp
from jax import lax

NY = 512
K = 128
STEPS = 3
LEVELS = 2
NCASE = 4
NX = 128


def draw_forcing(key, part):
    shape = (NCASE, NX, NY, K)
    values = jax.random.truncated_normal(jax.random.fold_in(key, 13), -6.0, 6.0, shape, jnp.float32)
    return values.astype(jnp.bfloat16)


def with_ends(drawn, key, smallest, high):
    longest = drawn.shape.index(max(drawn.shape))
    spots = []
    for shift in (0, 1):
        where = [jax.random.randint(jax.random.fold_in(key, axis), (), 0, length) for axis, length in enumerate(drawn.shape)]
        where[longest] = (where[longest] + shift) % drawn.shape[longest]
        spots.append(tuple(where))
    return drawn.at[spots[0]].set(smallest).at[spots[1]].set(high)


def shard_levels(key, shape, cuts, least, top_value):
    def one(axis_at, parts):
        heights = jax.random.uniform(jax.random.fold_in(jax.random.fold_in(key, 6), axis_at), (parts,), jnp.float32, least / len(cuts), top_value / len(cuts))
        return jnp.repeat(jnp.exp(heights), shape[axis_at] // parts).reshape((-1,) + (1,) * (len(shape) - axis_at - 1))

    factor_of = one(*cuts[0])
    for cut in cuts[1:]:
        factor_of = factor_of * one(*cut)
    return factor_of


def setup_inputs(seed: int = 0) -> dict:
    seeds = jax.random.split(jax.random.key(seed), 5)
    return {
        "forcing": draw_forcing(jax.random.fold_in(seeds[4], 71), 0),
        "permeability": jnp.clip(jnp.exp(math.log(1.0) - 2.9957323 * jax.random.uniform(seeds[1], (NCASE, NX, NY), jnp.float32) ** shard_levels(seeds[1], (NCASE, NX, NY), ((0, 4), (1, 8)), -0.2, 0.2)), 0.05, 1.0),
        "merge_weights": with_ends(jax.random.randint(seeds[2], (NCASE,), 4, 7), jax.random.fold_in(seeds[2], 1), 4, 6).astype(jnp.int32),
        "start_codes": with_ends(jax.random.randint(seeds[3], (LEVELS, 2 * K, K), -7, 8), jax.random.fold_in(seeds[3], 1), -7, 7).astype(jnp.int32),
    }


def stencil_step(ext_field, ext_perm):
    wide_field = jnp.pad(ext_field, ((0, 0), (1, 1), (0, 0)))
    wide_perm = jnp.pad(ext_perm, ((0, 0), (1, 1)))
    center = ext_field[1:-1]
    perm_mid = ext_perm[1:-1]
    t_north = 0.5 * (perm_mid + ext_perm[2:])
    t_south = 0.5 * (perm_mid + ext_perm[:-2])
    t_east = 0.5 * (perm_mid + wide_perm[1:-1, 2:])
    t_west = 0.5 * (perm_mid + wide_perm[1:-1, :-2])
    flux = t_north[:, :, None] * (ext_field[2:] - center)
    flux = flux + t_south[:, :, None] * (ext_field[:-2] - center)
    flux = flux + t_east[:, :, None] * (wide_field[1:-1, 2:] - center)
    flux = flux + t_west[:, :, None] * (wide_field[1:-1, :-2] - center)
    return center + 0.24 * flux

def merge(own, other, start_code):
    cells = NX * NY
    stacked = jnp.concatenate([own, other], 1)
    gram = jnp.dot(stacked.T.astype(jnp.float32), stacked.astype(jnp.float32), preferred_element_type=jnp.float32)
    start = start_code.astype(jnp.float32)
    first = jnp.dot(gram, start, precision=lax.Precision.HIGHEST) / cells
    second = jnp.dot(gram, first, precision=lax.Precision.HIGHEST) / cells
    coeff = second.astype(jnp.bfloat16)
    compressed = jnp.dot(stacked.astype(jnp.float32), coeff.astype(jnp.float32), preferred_element_type=jnp.float32)
    inner = jnp.dot(compressed.T, compressed, precision=lax.Precision.HIGHEST)
    factor = jnp.linalg.cholesky(inner)
    solved = lax.linalg.triangular_solve(factor, compressed, left_side=False, lower=True, transpose_a=True)
    return (math.sqrt(cells) * solved).astype(jnp.bfloat16)

def reference(forcing, permeability, merge_weights, start_codes):
    bases = []
    for group in range(NCASE):
        field = forcing[group].astype(jnp.float32)
        ext_perm = jnp.pad(permeability[group], ((1, 1), (0, 0)))
        for step in range(STEPS):
            field = stencil_step(jnp.pad(field, ((1, 1), (0, 0), (0, 0))), ext_perm)
        weight = jnp.sqrt(merge_weights[group].astype(jnp.float32))
        bases.append((field * weight).astype(jnp.bfloat16).reshape(NX * NY, K))
    for level in range(LEVELS):
        updated = []
        for group in range(NCASE):
            other = group ^ 1 << level
            updated.append(merge(bases[group], bases[other], start_codes[level]))
        bases = updated
    return jnp.stack(bases)
```

```python
import functools
import math

import jax
import jax.numpy as jnp
from jax import lax
from jax.experimental import pallas as pl
from jax.experimental.pallas import tpu as pltpu
from jax.sharding import PartitionSpec as P

STEPS = 3
LEVELS = 2
PAD = 8
PANEL = 16
HIGHEST = lax.Precision.HIGHEST
MESH = pl.DeviceIdType.MESH
VMEM_BYTES = 60 * 2**20


def peers(axis, size):
    me = lax.axis_index(axis)
    return [{axis: lax.rem(me + k, size)} for k in range(size)]


def barrier(*axes):
    sem = pltpu.get_barrier_semaphore()
    count = 0
    for axis, size in axes:
        for device in peers(axis, size)[1:]:
            pl.semaphore_signal(sem, inc=1, device_id=device, device_id_type=MESH)
            count += 1
    pl.semaphore_wait(sem, count)


def remote(src, dst, send, recv, device):
    return pltpu.make_async_remote_copy(
        src_ref=src, dst_ref=dst, send_sem=send, recv_sem=recv, device_id=device, device_id_type=MESH
    )


def front_kernel(
    cases, tiles, f_ref, a_ref, b_ref, weight_ref, s_ref, gram_ref,
    halo, u, w, wide_a, wide_b, out, flat, part, case_in, acc, tile_in,
    halo_send, halo_recv, s_send, s_recv, cs_send, cs_recv, ts_send, ts_recv, tg_send, tg_recv, cg_send, cg_recv,
):
    rows, ny, lanes = f_ref.shape
    ext = rows + 2 * STEPS
    quarter = rows // cases
    case, tile = lax.axis_index("case"), lax.axis_index("tile")
    case_peers, tile_peers = peers("case", cases), peers("tile", tiles)
    chunk = 128
    barrier(("case", cases), ("tile", tiles))

    back = remote(f_ref.at[pl.ds(0, STEPS)], halo.at[1], halo_send.at[0], halo_recv.at[1], {"tile": tile - 1})
    ahead = remote(f_ref.at[pl.ds(rows - STEPS, STEPS)], halo.at[0], halo_send.at[1], halo_recv.at[0], {"tile": tile + 1})

    @pl.when(tile > 0)
    def _():
        back.start()

    @pl.when(tile < tiles - 1)
    def _():
        ahead.start()

    for slot in range(2):
        @pl.loop(0, ext)
        def _(r):
            zeros = jnp.zeros((PAD, lanes), jnp.float32)
            u[slot, r, pl.ds(0, PAD)] = zeros
            u[slot, r, pl.ds(PAD + ny, PAD)] = zeros
            w[slot, r, pl.ds(0, PAD)] = zeros
            w[slot, r, pl.ds(PAD + ny, PAD)] = zeros

    @pl.loop(0, ny // 64)
    def _(y):
        ys = pl.ds(pl.multiple_of(y * 64, 64), 64)
        col_a, col_b = a_ref[ys, :], b_ref[ys, :]
        for r in range(ext):
            wide_a[r, ys] = jnp.broadcast_to(col_a[:, r : r + 1], (64, lanes))
            wide_b[r, ys] = jnp.broadcast_to(col_b[:, r : r + 1], (64, lanes))

    def take(r, load):
        for y in range(0, ny, chunk):
            value = load(y).astype(jnp.float32)
            u[0, r, pl.ds(PAD + y, chunk)] = value
            w[0, r, pl.ds(PAD + y, chunk)] = value * wide_a[r, pl.ds(y, chunk)]

    @pl.loop(0, rows)
    def _(r):
        take(r + STEPS, lambda y: f_ref[r, pl.ds(y, chunk)])

    @pl.when(tile > 0)
    def _():
        back.wait_send()
        ahead.wait_recv()

    @pl.when(tile < tiles - 1)
    def _():
        ahead.wait_send()
        back.wait_recv()

    @pl.when(tile == 0)
    def _():
        halo[0] = jnp.zeros((STEPS, ny, lanes), halo.dtype)

    @pl.when(tile == tiles - 1)
    def _():
        halo[1] = jnp.zeros((STEPS, ny, lanes), halo.dtype)

    @pl.loop(0, STEPS)
    def _(r):
        take(r, lambda y: halo[0, r, pl.ds(y, chunk)])
        take(r + STEPS + rows, lambda y: halo[1, r, pl.ds(y, chunk)])

    def stepped(src, r, y):
        at = pl.ds(PAD + y, chunk)
        sides = (r + 1, at), (r - 1, at), (r, pl.ds(PAD + y + 1, chunk)), (r, pl.ds(PAD + y - 1, chunk))
        total_u = sum(u[src, i, j] for i, j in sides[1:]) + u[src, sides[0][0], sides[0][1]]
        total_w = sum(w[src, i, j] for i, j in sides[1:]) + w[src, sides[0][0], sides[0][1]]
        ys = pl.ds(y, chunk)
        coef = wide_a[r, ys]
        return wide_b[r, ys] * u[src, r, at] + coef * total_u + total_w, coef

    for step in range(STEPS - 1):
        src, dst = step % 2, (step + 1) % 2

        @pl.loop(step + 1, ext - step - 1)
        def _(r):
            inside = ((r >= STEPS) | (tile > 0)) & ((r < STEPS + rows) | (tile < tiles - 1))
            mask = jnp.where(inside, 1.0, 0.0)
            for y in range(0, ny, chunk):
                value, coef = stepped(src, r, y)
                value = value * mask
                u[dst, r, pl.ds(PAD + y, chunk)] = value
                w[dst, r, pl.ds(PAD + y, chunk)] = value * coef

    last = (STEPS - 1) % 2
    weight = weight_ref[0:1, :]
    copies = []
    for k in [k for k in range(cases) if k] + [0]:
        first = lax.rem(case + k, cases) * quarter

        @pl.loop(0, quarter)
        def _(i):
            for y in range(0, ny, chunk):
                value = (stepped(last, first + i + STEPS, y)[0] * weight).astype(jnp.bfloat16)
                if k:
                    out[k, i, pl.ds(y, chunk)] = value
                else:
                    s_ref[case, i, pl.ds(y, chunk)] = value

        if k:
            copy = remote(out.at[k], s_ref.at[case], s_send.at[k], s_recv.at[k], case_peers[k])
            copy.start()
            copies.append(copy)
    for copy in copies:
        copy.wait()

    block = 0
    snaps = [s_ref[g].reshape(quarter * ny, lanes) for g in range(cases)]
    for g in range(cases):
        right = jnp.concatenate(snaps[g:], 1)
        terms = lax.dot_general(snaps[g], right, (((0,), (0,)), ((), ())), preferred_element_type=jnp.float32)
        for h in range(cases - g):
            flat[block * lanes : (block + 1) * lanes, :] = terms[:, h * lanes : (h + 1) * lanes]
            block += 1
    share = part.shape[2]
    for i in range(cases * tiles):
        part[i // tiles, i % tiles] = flat[i * share : (i + 1) * share, :]

    def exchange(devices, source, target, send, recv):
        started = [remote(source(k), target(k), send.at[k], recv.at[k], devices[k]) for k in range(1, len(devices))]
        for copy in started:
            copy.start()
        for copy in started:
            copy.wait()

    exchange(
        case_peers, lambda k: part.at[lax.rem(case + k, cases)], lambda k: case_in.at[k], cs_send, cs_recv
    )
    total = part[case]
    for k in range(1, cases):
        total = total + case_in[k]
    acc[...] = total
    exchange(
        tile_peers, lambda k: acc.at[lax.rem(tile + k, tiles)], lambda k: tile_in.at[k], ts_send, ts_recv
    )
    total = acc[tile]
    for k in range(1, tiles):
        total = total + tile_in[k]
    gram_ref[case, tile] = total
    exchange(tile_peers, lambda k: gram_ref.at[case, tile], lambda k: gram_ref.at[case, tile], tg_send, tg_recv)
    exchange(case_peers, lambda k: gram_ref.at[case], lambda k: gram_ref.at[case], cg_send, cg_recv)


def front(cases, tiles, forcing, coef_a, coef_b, weight):
    rows, ny, lanes = forcing.shape
    ext, quarter = rows + 2 * STEPS, rows // cases
    total = cases * (cases + 1) // 2 * lanes
    share = total // (cases * tiles)
    f32, bf16 = jnp.float32, jnp.bfloat16
    vmem = pl.BlockSpec(memory_space=pltpu.VMEM)
    dma = pltpu.SemaphoreType.DMA
    return pl.pallas_call(
        functools.partial(front_kernel, cases, tiles),
        out_shape=(
            jax.ShapeDtypeStruct((cases, quarter, ny, lanes), bf16),
            jax.ShapeDtypeStruct((cases, tiles, share, lanes), f32),
        ),
        in_specs=[vmem] * 4,
        out_specs=(vmem, vmem),
        scratch_shapes=[
            pltpu.VMEM((2, STEPS, ny, lanes), bf16),
            pltpu.VMEM((2, ext, ny + 2 * PAD, lanes), f32),
            pltpu.VMEM((2, ext, ny + 2 * PAD, lanes), f32),
            pltpu.VMEM((ext, ny, lanes), f32),
            pltpu.VMEM((ext, ny, lanes), f32),
            pltpu.VMEM((cases, quarter, ny, lanes), bf16),
            pltpu.VMEM((total, lanes), f32),
            pltpu.VMEM((cases, tiles, share, lanes), f32),
            pltpu.VMEM((cases, tiles, share, lanes), f32),
            pltpu.VMEM((tiles, share, lanes), f32),
            pltpu.VMEM((tiles, share, lanes), f32),
            dma((2,)), dma((2,)),
            dma((cases,)), dma((cases,)),
            dma((cases,)), dma((cases,)),
            dma((tiles,)), dma((tiles,)),
            dma((tiles,)), dma((tiles,)),
            dma((cases,)), dma((cases,)),
        ],
        compiler_params=pltpu.CompilerParams(collective_id=0, has_side_effects=True, vmem_limit_bytes=VMEM_BYTES),
    )(forcing, coef_a, coef_b, weight)


def dot(left, right):
    return jnp.dot(left, right, precision=HIGHEST, preferred_element_type=jnp.float32)


def dot_rows(left, right):
    return lax.dot_general(
        left, right, (((0,), (0,)), ((), ())), precision=HIGHEST, preferred_element_type=jnp.float32
    )


def inverse_factors(work, inners):
    count, size = len(inners), inners[0].shape[0]
    eye = (
        lax.broadcasted_iota(jnp.int32, (size, size), 0) == lax.broadcasted_iota(jnp.int32, (size, size), 1)
    ).astype(jnp.float32)
    for b in range(count):
        work[b, :, :size] = inners[b]
        work[b, :, size:] = eye
    index = lax.broadcasted_iota(jnp.int32, (count, PANEL, 1), 1)
    for top in range(0, size, PANEL):
        panel = work[:, top : top + PANEL, :]
        scale = jnp.ones((count, PANEL, 1), jnp.float32)
        for i in range(PANEL):
            column = panel[:, :, top + i : top + i + 1]
            root = lax.rsqrt(column[:, i : i + 1, :])
            scale = jnp.where(index == i, root, scale)
            factor = jnp.where(index > i, column * (root * root), 0.0)
            panel = panel - factor * panel[:, i : i + 1, :]
        panel = panel * scale
        work[:, top : top + PANEL, :] = panel
        below = top + PANEL
        if below < size:
            for b in range(count):
                lead = panel[b][:, :size]
                update = dot_rows(lead, panel[b])
                work[b, below:, :] = work[b, below:, :] - update[below:, :]
    return [work[b, :, size:] for b in range(count)]


def solve_kernel(cells, gram_ref, code_ref, out_ref, work):
    cases, lanes = out_ref.shape[0], out_ref.shape[2]
    grams, block = {}, 0
    for g in range(cases):
        for h in range(g, cases):
            value = gram_ref[block]
            grams[g, h] = value
            if h != g:
                grams[h, g] = value.T
            block += 1

    def joined(left, right):
        return jnp.concatenate([jnp.concatenate([grams[g, h] for h in right], 1) for g in left], 0)

    bases = {c: ([c], None) for c in range(cases)}
    for level in range(LEVELS):
        start = code_ref[level].astype(jnp.float32)
        coeffs, inners = [], []
        for c in range(cases):
            pair = (c, c ^ 2**level)
            if level == 0:
                gram = joined(pair, pair)
            else:
                rows = []
                for g in pair:
                    parts = [
                        dot_rows(bases[g][1], dot(joined(bases[g][0], bases[h][0]), bases[h][1])) for h in pair
                    ]
                    rows.append(jnp.concatenate(parts, 1))
                gram = jnp.concatenate(rows, 0)
            first = dot(gram, start) / cells
            second = dot(gram, first) / cells
            coeff = second.astype(jnp.bfloat16).astype(jnp.float32)
            coeffs.append(coeff)
            inners.append(dot_rows(coeff, dot(gram, coeff)))
        inverses = inverse_factors(work, inners)
        updated = {}
        for c in range(cases):
            p = c ^ 2**level
            turned = lax.dot_general(
                coeffs[c], inverses[c], (((1,), (1,)), ((), ())), precision=HIGHEST, preferred_element_type=jnp.float32
            ) * math.sqrt(cells)
            if level == 0:
                updated[c] = ([c, p], turned)
            else:
                head, tail = turned[:lanes], turned[lanes:]
                updated[c] = (
                    bases[c][0] + bases[p][0],
                    jnp.concatenate([dot(bases[c][1], head), dot(bases[p][1], tail)], 0),
                )
        bases = updated
    for c in range(cases):
        groups, matrix = bases[c]
        for i, g in enumerate(groups):
            out_ref[c, g * lanes : (g + 1) * lanes, :] = matrix[i * lanes : (i + 1) * lanes].astype(out_ref.dtype)


def solve(cases, cells, grams, codes):
    lanes = grams.shape[-1]
    vmem = pl.BlockSpec(memory_space=pltpu.VMEM)
    return pl.pallas_call(
        functools.partial(solve_kernel, cells),
        out_shape=jax.ShapeDtypeStruct((cases, cases * lanes, lanes), jnp.bfloat16),
        in_specs=[vmem] * 2,
        out_specs=vmem,
        scratch_shapes=[pltpu.VMEM((cases, lanes, 2 * lanes), jnp.float32)],
        compiler_params=pltpu.CompilerParams(vmem_limit_bytes=VMEM_BYTES),
    )(grams, codes)


def back_kernel(cases, s_ref, m_ref, out_ref, buffer, send, recv):
    case = lax.axis_index("case")
    case_peers = peers("case", cases)
    cells = s_ref.shape[1]
    chunk = 512
    barrier(("case", cases))
    copies = []
    for k in [k for k in range(cases) if k] + [0]:
        matrix = m_ref[lax.rem(case + k, cases)]

        @pl.loop(0, cells // chunk)
        def _(i):
            at = pl.ds(pl.multiple_of(i * chunk, chunk), chunk)
            left = jnp.concatenate([s_ref[g, at, :] for g in range(cases)], 1)
            value = jnp.dot(left, matrix, preferred_element_type=jnp.float32).astype(out_ref.dtype)
            if k:
                buffer[k, at, :] = value
            else:
                out_ref[case, at, :] = value

        if k:
            copy = remote(buffer.at[k], out_ref.at[case], send.at[k], recv.at[k], case_peers[k])
            copy.start()
            copies.append(copy)
    for copy in copies:
        copy.wait()


def back(cases, snaps, matrices):
    vmem = pl.BlockSpec(memory_space=pltpu.VMEM)
    return pl.pallas_call(
        functools.partial(back_kernel, cases),
        out_shape=jax.ShapeDtypeStruct(snaps.shape, jnp.bfloat16),
        in_specs=[vmem] * 2,
        out_specs=vmem,
        scratch_shapes=[
            pltpu.VMEM(snaps.shape, jnp.bfloat16),
            pltpu.SemaphoreType.DMA((cases,)),
            pltpu.SemaphoreType.DMA((cases,)),
        ],
        compiler_params=pltpu.CompilerParams(collective_id=1, has_side_effects=True, vmem_limit_bytes=VMEM_BYTES),
    )(snaps, matrices)


def per_device(cases, tiles, forcing, permeability, merge_weights, start_codes):
    _, rows, ny, lanes = forcing.shape
    perm = permeability[0]
    before = lax.ppermute(perm[rows - STEPS :], "tile", [(i, i + 1) for i in range(tiles - 1)])
    after = lax.ppermute(perm[:STEPS], "tile", [(i + 1, i) for i in range(tiles - 1)])
    ext = jnp.concatenate([before, perm, after], 0)
    wide = jnp.pad(ext, 1)
    around = wide[2:, 1:-1] + wide[:-2, 1:-1] + wide[1:-1, 2:] + wide[1:-1, :-2]
    coef_a = 0.12 * ext
    coef_b = 1.0 - 0.12 * (4.0 * ext + around)
    widen = lambda value: jnp.pad(value, ((0, lanes - value.shape[0]), (0, 0))).T
    weight = jnp.broadcast_to(jnp.sqrt(merge_weights[0].astype(jnp.float32)), (8, lanes))
    snaps, grams = front(cases, tiles, forcing[0], widen(coef_a), widen(coef_b), weight)
    cells = rows * tiles * ny
    matrices = solve(cases, cells, grams.reshape(-1, lanes, lanes), start_codes)
    basis = back(cases, snaps.reshape(cases, -1, lanes), matrices)
    return basis.reshape(1, -1, lanes)


def solution(mesh):
    placed = (P("case", "tile", None, None), P("case", "tile", None), P("case"), P())
    return jax.shard_map(
        functools.partial(per_device, mesh.shape["case"], mesh.shape["tile"]),
        mesh=mesh, in_specs=placed, out_specs=P("case", "tile", None), check_vma=False,
    )
```

```python
import functools
import math

import jax
import jax.numpy as jnp
from jax import lax
from jax.experimental import pallas as pl
from jax.experimental.pallas import tpu as pltpu
from jax.sharding import PartitionSpec as P

STEPS = 3
LEVELS = 2
PAD = 8
PANEL = 16
GROUP = 4
HIGHEST = lax.Precision.HIGHEST
MESH = pl.DeviceIdType.MESH
VMEM_BYTES = 60 * 2**20


def peers(axis, size):
    me = lax.axis_index(axis)
    return [{axis: lax.rem(me + k, size)} for k in range(size)]


def barrier(*axes):
    sem = pltpu.get_barrier_semaphore()
    count = 0
    for axis, size in axes:
        for device in peers(axis, size)[1:]:
            pl.semaphore_signal(sem, inc=1, device_id=device, device_id_type=MESH)
            count += 1
    pl.semaphore_wait(sem, count)


def remote(src, dst, send, recv, device):
    return pltpu.make_async_remote_copy(
        src_ref=src, dst_ref=dst, send_sem=send, recv_sem=recv, device_id=device, device_id_type=MESH
    )


def front_kernel(
    cases, tiles, f_ref, p_ref, weight_ref, s_ref, gram_ref,
    halo, p_ext, p_turned, u, w, wide_a, wide_b, out, flat, part, case_in, acc, tile_in,
    halo_send, halo_recv, p_send, p_recv, s_send, s_recv, cs_send, cs_recv, ts_send, ts_recv, tg_send, tg_recv, cg_send, cg_recv,
):
    rows, ny, lanes = f_ref.shape
    ext = rows + 2 * STEPS
    quarter = rows // cases
    case, tile = lax.axis_index("case"), lax.axis_index("tile")
    case_peers, tile_peers = peers("case", cases), peers("tile", tiles)
    chunk = 128
    barrier(("case", cases), ("tile", tiles))

    back = remote(f_ref.at[pl.ds(0, STEPS)], halo.at[1], halo_send.at[0], halo_recv.at[1], {"tile": tile - 1})
    ahead = remote(f_ref.at[pl.ds(rows - STEPS, STEPS)], halo.at[0], halo_send.at[1], halo_recv.at[0], {"tile": tile + 1})

    p_back = remote(
        p_ref.at[pl.ds(0, PAD)], p_ext.at[pl.ds(PAD + rows, PAD)], p_send.at[0], p_recv.at[1], {"tile": tile - 1}
    )
    p_ahead = remote(
        p_ref.at[pl.ds(rows - PAD, PAD)], p_ext.at[pl.ds(0, PAD)], p_send.at[1], p_recv.at[0], {"tile": tile + 1}
    )

    @pl.when(tile > 0)
    def _():
        p_back.start()
        back.start()

    @pl.when(tile < tiles - 1)
    def _():
        p_ahead.start()
        ahead.start()

    @pl.when(tile == 0)
    def _():
        p_ext[0:PAD] = jnp.zeros((PAD, ny), jnp.float32)

    @pl.when(tile == tiles - 1)
    def _():
        p_ext[PAD + rows : 2 * PAD + rows] = jnp.zeros((PAD, ny), jnp.float32)

    p_ext[PAD : PAD + rows] = p_ref[...]
    p_ext[2 * PAD + rows :] = jnp.zeros((lanes - 2 * PAD - rows, ny), jnp.float32)
    p_turned[0:PAD] = jnp.zeros((PAD, lanes), jnp.float32)
    p_turned[PAD + ny :] = jnp.zeros((PAD, lanes), jnp.float32)

    for slot in range(2):
        @pl.loop(0, ext)
        def _(r):
            zeros = jnp.zeros((PAD, lanes), jnp.float32)
            u[slot, r, pl.ds(0, PAD)] = zeros
            u[slot, r, pl.ds(PAD + ny, PAD)] = zeros
            w[slot, r, pl.ds(0, PAD)] = zeros
            w[slot, r, pl.ds(PAD + ny, PAD)] = zeros

    @pl.when(tile > 0)
    def _():
        p_back.wait_send()
        p_ahead.wait_recv()

    @pl.when(tile < tiles - 1)
    def _():
        p_ahead.wait_send()
        p_back.wait_recv()

    for y in range(0, ny, lanes):
        p_turned[pl.ds(PAD + y, lanes)] = p_ext[:, y : y + lanes].T
    for y in range(0, ny, 64):
        mid = p_turned[pl.ds(PAD + y, 64)]
        around = p_turned[pl.ds(PAD + y + 1, 64)] + p_turned[pl.ds(PAD + y - 1, 64)]
        around = around + (pltpu.roll(mid, 1, 1) + pltpu.roll(mid, lanes - 1, 1))
        col_a = 0.12 * mid
        col_b = 1.0 - 0.12 * (4.0 * mid + around)
        for r in range(ext):
            at = r + PAD - STEPS
            wide_a[r, pl.ds(y, 64)] = jnp.broadcast_to(col_a[:, at : at + 1], (64, lanes))
            wide_b[r, pl.ds(y, 64)] = jnp.broadcast_to(col_b[:, at : at + 1], (64, lanes))

    def take(r, load):
        for y in range(0, ny, chunk):
            value = load(y).astype(jnp.float32)
            u[0, r, pl.ds(PAD + y, chunk)] = value
            w[0, r, pl.ds(PAD + y, chunk)] = value * wide_a[r, pl.ds(y, chunk)]

    @pl.loop(0, rows)
    def _(r):
        take(r + STEPS, lambda y: f_ref[r, pl.ds(y, chunk)])

    @pl.when(tile > 0)
    def _():
        back.wait_send()
        ahead.wait_recv()

    @pl.when(tile < tiles - 1)
    def _():
        ahead.wait_send()
        back.wait_recv()

    @pl.when(tile == 0)
    def _():
        halo[0] = jnp.zeros((STEPS, ny, lanes), halo.dtype)

    @pl.when(tile == tiles - 1)
    def _():
        halo[1] = jnp.zeros((STEPS, ny, lanes), halo.dtype)

    @pl.loop(0, STEPS)
    def _(r):
        take(r, lambda y: halo[0, r, pl.ds(y, chunk)])
        take(r + STEPS + rows, lambda y: halo[1, r, pl.ds(y, chunk)])

    def stepped(src, r, y):
        at = pl.ds(PAD + y, chunk)
        sides = (r + 1, at), (r - 1, at), (r, pl.ds(PAD + y + 1, chunk)), (r, pl.ds(PAD + y - 1, chunk))
        total_u = sum(u[src, i, j] for i, j in sides[1:]) + u[src, sides[0][0], sides[0][1]]
        total_w = sum(w[src, i, j] for i, j in sides[1:]) + w[src, sides[0][0], sides[0][1]]
        ys = pl.ds(y, chunk)
        coef = wide_a[r, ys]
        return wide_b[r, ys] * u[src, r, at] + coef * total_u + total_w, coef

    for step in range(STEPS - 1):
        src, dst = step % 2, (step + 1) % 2

        @pl.loop(step + 1, ext - step - 1)
        def _(r):
            inside = ((r >= STEPS) | (tile > 0)) & ((r < STEPS + rows) | (tile < tiles - 1))
            mask = jnp.where(inside, 1.0, 0.0)
            for y in range(0, ny, chunk):
                value, coef = stepped(src, r, y)
                value = value * mask
                u[dst, r, pl.ds(PAD + y, chunk)] = value
                w[dst, r, pl.ds(PAD + y, chunk)] = value * coef

    last = (STEPS - 1) % 2
    weight = jnp.sqrt(jnp.full((1, lanes), weight_ref[0].astype(jnp.float32)))
    copies = []
    for k in [k for k in range(cases) if k] + [0]:
        first = lax.rem(case + k, cases) * quarter

        @pl.loop(0, quarter)
        def _(i):
            for y in range(0, ny, chunk):
                value = (stepped(last, first + i + STEPS, y)[0] * weight).astype(jnp.bfloat16)
                if k:
                    out[k, i, pl.ds(y, chunk)] = value
                else:
                    s_ref[case, i, pl.ds(y, chunk)] = value

        if k:
            copy = remote(out.at[k], s_ref.at[case], s_send.at[k], s_recv.at[k], case_peers[k])
            copy.start()
            copies.append(copy)
    for copy in copies:
        copy.wait()

    block = 0
    snaps = [s_ref[g].reshape(quarter * ny, lanes) for g in range(cases)]
    for g in range(cases):
        right = jnp.concatenate(snaps[g:], 1)
        terms = lax.dot_general(snaps[g], right, (((0,), (0,)), ((), ())), preferred_element_type=jnp.float32)
        for h in range(cases - g):
            flat[block * lanes : (block + 1) * lanes, :] = terms[:, h * lanes : (h + 1) * lanes]
            block += 1
    share = part.shape[2]
    for i in range(cases * tiles):
        part[i // tiles, i % tiles] = flat[i * share : (i + 1) * share, :]

    def exchange(devices, source, target, send, recv):
        started = [remote(source(k), target(k), send.at[k], recv.at[k], devices[k]) for k in range(1, len(devices))]
        for copy in started:
            copy.start()
        for copy in started:
            copy.wait()

    exchange(
        case_peers, lambda k: part.at[lax.rem(case + k, cases)], lambda k: case_in.at[k], cs_send, cs_recv
    )
    total = part[case]
    for k in range(1, cases):
        total = total + case_in[k]
    acc[...] = total
    exchange(
        tile_peers, lambda k: acc.at[lax.rem(tile + k, tiles)], lambda k: tile_in.at[k], ts_send, ts_recv
    )
    total = acc[tile]
    for k in range(1, tiles):
        total = total + tile_in[k]
    gram_ref[case, tile] = total
    exchange(tile_peers, lambda k: gram_ref.at[case, tile], lambda k: gram_ref.at[case, tile], tg_send, tg_recv)
    exchange(case_peers, lambda k: gram_ref.at[case], lambda k: gram_ref.at[case], cg_send, cg_recv)


def front(cases, tiles, forcing, permeability, merge_weights):
    rows, ny, lanes = forcing.shape
    ext, quarter = rows + 2 * STEPS, rows // cases
    total = cases * (cases + 1) // 2 * lanes
    share = total // (cases * tiles)
    f32, bf16 = jnp.float32, jnp.bfloat16
    vmem = pl.BlockSpec(memory_space=pltpu.VMEM)
    dma = pltpu.SemaphoreType.DMA
    return pl.pallas_call(
        functools.partial(front_kernel, cases, tiles),
        out_shape=(
            jax.ShapeDtypeStruct((cases, quarter, ny, lanes), bf16),
            jax.ShapeDtypeStruct((cases, tiles, share, lanes), f32),
        ),
        in_specs=[vmem, vmem, pl.BlockSpec(memory_space=pltpu.SMEM)],
        out_specs=(vmem, vmem),
        scratch_shapes=[
            pltpu.VMEM((2, STEPS, ny, lanes), bf16),
            pltpu.VMEM((lanes, ny), f32),
            pltpu.VMEM((ny + 2 * PAD, lanes), f32),
            pltpu.VMEM((2, ext, ny + 2 * PAD, lanes), f32),
            pltpu.VMEM((2, ext, ny + 2 * PAD, lanes), f32),
            pltpu.VMEM((ext, ny, lanes), f32),
            pltpu.VMEM((ext, ny, lanes), f32),
            pltpu.VMEM((cases, quarter, ny, lanes), bf16),
            pltpu.VMEM((total, lanes), f32),
            pltpu.VMEM((cases, tiles, share, lanes), f32),
            pltpu.VMEM((cases, tiles, share, lanes), f32),
            pltpu.VMEM((tiles, share, lanes), f32),
            pltpu.VMEM((tiles, share, lanes), f32),
            dma((2,)), dma((2,)),
            dma((2,)), dma((2,)),
            dma((cases,)), dma((cases,)),
            dma((cases,)), dma((cases,)),
            dma((tiles,)), dma((tiles,)),
            dma((tiles,)), dma((tiles,)),
            dma((cases,)), dma((cases,)),
        ],
        compiler_params=pltpu.CompilerParams(collective_id=0, has_side_effects=True, vmem_limit_bytes=VMEM_BYTES),
    )(forcing, permeability, merge_weights)


def dot(left, right):
    return jnp.dot(left, right, precision=HIGHEST, preferred_element_type=jnp.float32)


def dot_rows(left, right):
    return lax.dot_general(
        left, right, (((0,), (0,)), ((), ())), precision=HIGHEST, preferred_element_type=jnp.float32
    )


def inverse_factors(work, inners):
    count, size = len(inners), inners[0].shape[0]
    eye = (
        lax.broadcasted_iota(jnp.int32, (size, size), 0) == lax.broadcasted_iota(jnp.int32, (size, size), 1)
    ).astype(jnp.float32)
    for b in range(count):
        work[b, :, :size] = inners[b]
        work[b, :, size:] = eye
    shape = (count, PANEL, size)
    index = lax.broadcasted_iota(jnp.int32, shape, 1)
    for top in range(0, size, PANEL):
        left = work[:, top : top + PANEL, :size]
        right = work[:, top : top + PANEL, size:]
        scale = jnp.ones(shape, jnp.float32)
        for group in range(0, PANEL, GROUP):
            at = top + group
            columns = [jnp.broadcast_to(left[:, :, at + j : at + j + 1], shape) for j in range(GROUP)]
            for j in range(GROUP):
                i = group + j
                root = lax.rsqrt(columns[j][:, i : i + 1, :])
                scale = jnp.where(index == i, root, scale)
                factor = jnp.where(index > i, columns[j] * (root * root), 0.0)
                for m in range(j + 1, GROUP):
                    columns[m] = columns[m] - factor * columns[m][:, i : i + 1, :]
                left = left - factor * left[:, i : i + 1, :]
                right = right - factor * right[:, i : i + 1, :]
        panel = jnp.concatenate([left * scale, right * scale], 2)
        work[:, top : top + PANEL, :] = panel
        below = top + PANEL
        if below < size:
            for b in range(count):
                lead = panel[b][:, :size]
                update = dot_rows(lead, panel[b])
                work[b, below:, :] = work[b, below:, :] - update[below:, :]
    return [work[b, :, size:] for b in range(count)]


def solve_kernel(cells, gram_ref, code_ref, out_ref, work):
    cases, lanes = out_ref.shape[0], out_ref.shape[2]
    grams, block = {}, 0
    for g in range(cases):
        for h in range(g, cases):
            value = gram_ref[block]
            grams[g, h] = value
            if h != g:
                grams[h, g] = value.T
            block += 1

    def joined(left, right):
        return jnp.concatenate([jnp.concatenate([grams[g, h] for h in right], 1) for g in left], 0)

    bases = {c: ([c], None) for c in range(cases)}
    for level in range(LEVELS):
        crossed = {}

        def cross(g, h):
            if (h, g) in crossed:
                return crossed[h, g].T
            if (g, h) not in crossed:
                value = dot(joined(bases[g][0], bases[h][0]), bases[h][1])
                crossed[g, h] = dot_rows(bases[g][1], value)
            return crossed[g, h]

        start = code_ref[level].astype(jnp.float32)
        coeffs, inners = [], []
        for c in range(cases):
            pair = (c, c ^ 2**level)
            if level == 0:
                gram = joined(pair, pair)
            else:
                rows = []
                for g in pair:
                    parts = [cross(g, h) for h in pair]
                    rows.append(jnp.concatenate(parts, 1))
                gram = jnp.concatenate(rows, 0)
            first = dot(gram, start) / cells
            second = dot(gram, first) / cells
            coeff = second.astype(jnp.bfloat16).astype(jnp.float32)
            coeffs.append(coeff)
            inners.append(dot_rows(coeff, dot(gram, coeff)))
        inverses = inverse_factors(work, inners)
        updated = {}
        for c in range(cases):
            p = c ^ 2**level
            turned = lax.dot_general(
                coeffs[c], inverses[c], (((1,), (1,)), ((), ())), precision=HIGHEST, preferred_element_type=jnp.float32
            ) * math.sqrt(cells)
            if level == 0:
                updated[c] = ([c, p], turned)
            else:
                head, tail = turned[:lanes], turned[lanes:]
                updated[c] = (
                    bases[c][0] + bases[p][0],
                    jnp.concatenate([dot(bases[c][1], head), dot(bases[p][1], tail)], 0),
                )
        bases = updated
    for c in range(cases):
        groups, matrix = bases[c]
        for i, g in enumerate(groups):
            out_ref[c, g * lanes : (g + 1) * lanes, :] = matrix[i * lanes : (i + 1) * lanes].astype(out_ref.dtype)


def solve(cases, cells, grams, codes):
    lanes = grams.shape[-1]
    vmem = pl.BlockSpec(memory_space=pltpu.VMEM)
    return pl.pallas_call(
        functools.partial(solve_kernel, cells),
        out_shape=jax.ShapeDtypeStruct((cases, cases * lanes, lanes), jnp.bfloat16),
        in_specs=[vmem] * 2,
        out_specs=vmem,
        scratch_shapes=[pltpu.VMEM((cases, lanes, 2 * lanes), jnp.float32)],
        compiler_params=pltpu.CompilerParams(vmem_limit_bytes=VMEM_BYTES),
    )(grams, codes)


def back_kernel(cases, s_ref, m_ref, out_ref, buffer, send, recv):
    case = lax.axis_index("case")
    case_peers = peers("case", cases)
    cells = s_ref.shape[1]
    pieces = send.shape[1]
    chunk = cells // pieces
    barrier(("case", cases))
    copies = []
    for i in range(pieces):
        at = pl.ds(i * chunk, chunk)
        left = jnp.concatenate([s_ref[g, at, :] for g in range(cases)], 1)
        for k in [k for k in range(cases) if k] + [0]:
            matrix = m_ref[lax.rem(case + k, cases)]
            value = jnp.dot(left, matrix, preferred_element_type=jnp.float32).astype(out_ref.dtype)
            if k:
                buffer[k, at, :] = value
                copy = remote(
                    buffer.at[k, at], out_ref.at[case, at], send.at[k, i], recv.at[k, i], case_peers[k]
                )
                copy.start()
                copies.append(copy)
            else:
                out_ref[case, at, :] = value
    for copy in copies:
        copy.wait()


def back(cases, snaps, matrices):
    vmem = pl.BlockSpec(memory_space=pltpu.VMEM)
    return pl.pallas_call(
        functools.partial(back_kernel, cases),
        out_shape=jax.ShapeDtypeStruct(snaps.shape, jnp.bfloat16),
        in_specs=[vmem] * 2,
        out_specs=vmem,
        scratch_shapes=[
            pltpu.VMEM(snaps.shape, jnp.bfloat16),
            pltpu.SemaphoreType.DMA((cases, 4)),
            pltpu.SemaphoreType.DMA((cases, 4)),
        ],
        compiler_params=pltpu.CompilerParams(collective_id=1, has_side_effects=True, vmem_limit_bytes=VMEM_BYTES),
    )(snaps, matrices)


def per_device(cases, tiles, forcing, permeability, merge_weights, start_codes):
    _, rows, ny, lanes = forcing.shape
    snaps, grams = front(cases, tiles, forcing[0], permeability[0], merge_weights)
    cells = rows * tiles * ny
    matrices = solve(cases, cells, grams.reshape(-1, lanes, lanes), start_codes)
    basis = back(cases, snaps.reshape(cases, -1, lanes), matrices)
    return basis.reshape(1, -1, lanes)


def solution(mesh):
    placed = (P("case", "tile", None, None), P("case", "tile", None), P("case"), P())
    return jax.shard_map(
        functools.partial(per_device, mesh.shape["case"], mesh.shape["tile"]),
        mesh=mesh, in_specs=placed, out_specs=P("case", "tile", None), check_vma=False,
    )
```

```python
import functools
import math

import jax
import jax.numpy as jnp
from jax import lax
from jax.experimental import pallas as pl
from jax.experimental.pallas import tpu as pltpu
from jax.sharding import PartitionSpec as P

STEPS = 3
LEVELS = 2
PAD = 8
PANEL = 16
GROUP = 4
HIGHEST = lax.Precision.HIGHEST
MESH = pl.DeviceIdType.MESH
VMEM_BYTES = 60 * 2**20


def peers(axis, size):
    me = lax.axis_index(axis)
    return [{axis: lax.rem(me + k, size)} for k in range(size)]


def barrier(*axes):
    sem = pltpu.get_barrier_semaphore()
    count = 0
    for axis, size in axes:
        for device in peers(axis, size)[1:]:
            pl.semaphore_signal(sem, inc=1, device_id=device, device_id_type=MESH)
            count += 1
    pl.semaphore_wait(sem, count)


def remote(src, dst, send, recv, device):
    return pltpu.make_async_remote_copy(
        src_ref=src, dst_ref=dst, send_sem=send, recv_sem=recv, device_id=device, device_id_type=MESH
    )


def front_kernel(
    cases, tiles, f_ref, p_ref, weight_ref, s_ref, gram_ref,
    halo, p_ext, p_turned, u, wide_a, wide_b, out, flat, part, core_in, core_sum, case_in, acc, chip_in,
    halo_send, halo_recv, p_send, p_recv, s_send, s_recv,
    rs_send, rs_recv, cs_send, cs_recv, ts_send, ts_recv, tg_send, tg_recv, cg_send, cg_recv, rg_send, rg_recv,
):
    rows, ny, lanes = f_ref.shape
    ext = rows + 2 * STEPS
    quarter = rows // cases
    case, tile = lax.axis_index("case"), lax.axis_index("tile")
    case_peers, tile_peers = peers("case", cases), peers("tile", tiles)
    chunk = 128
    barrier(("case", cases), ("tile", tiles))

    back = remote(f_ref.at[pl.ds(0, STEPS)], halo.at[1], halo_send.at[0], halo_recv.at[1], {"tile": tile - 1})
    ahead = remote(f_ref.at[pl.ds(rows - STEPS, STEPS)], halo.at[0], halo_send.at[1], halo_recv.at[0], {"tile": tile + 1})

    p_back = remote(
        p_ref.at[pl.ds(0, PAD)], p_ext.at[pl.ds(PAD + rows, PAD)], p_send.at[0], p_recv.at[1], {"tile": tile - 1}
    )
    p_ahead = remote(
        p_ref.at[pl.ds(rows - PAD, PAD)], p_ext.at[pl.ds(0, PAD)], p_send.at[1], p_recv.at[0], {"tile": tile + 1}
    )

    @pl.when(tile > 0)
    def _():
        p_back.start()
        back.start()

    @pl.when(tile < tiles - 1)
    def _():
        p_ahead.start()
        ahead.start()

    @pl.when(tile == 0)
    def _():
        p_ext[0:PAD] = jnp.zeros((PAD, ny), jnp.float32)

    @pl.when(tile == tiles - 1)
    def _():
        p_ext[PAD + rows : 2 * PAD + rows] = jnp.zeros((PAD, ny), jnp.float32)

    p_ext[PAD : PAD + rows] = p_ref[...]
    p_ext[2 * PAD + rows :] = jnp.zeros((lanes - 2 * PAD - rows, ny), jnp.float32)
    p_turned[0:PAD] = jnp.zeros((PAD, lanes), jnp.float32)
    p_turned[PAD + ny :] = jnp.zeros((PAD, lanes), jnp.float32)

    @pl.loop(0, ext)
    def _(r):
        zeros = jnp.zeros((PAD, lanes), jnp.float32)
        for at in (pl.ds(0, PAD), pl.ds(PAD + ny, PAD)):
            wide_a[r, at] = zeros
            for slot in range(STEPS):
                u[slot, r, at] = zeros

    @pl.when(tile > 0)
    def _():
        p_back.wait_send()
        p_ahead.wait_recv()

    @pl.when(tile < tiles - 1)
    def _():
        p_ahead.wait_send()
        p_back.wait_recv()

    for y in range(0, ny, lanes):
        p_turned[pl.ds(PAD + y, lanes)] = p_ext[:, y : y + lanes].T
    for y in range(0, ny, 64):
        mid = p_turned[pl.ds(PAD + y, 64)]
        around = p_turned[pl.ds(PAD + y + 1, 64)] + p_turned[pl.ds(PAD + y - 1, 64)]
        around = around + (pltpu.roll(mid, 1, 1) + pltpu.roll(mid, lanes - 1, 1))
        col_a = 0.12 * mid
        col_b = 1.0 - 0.12 * (4.0 * mid + around)
        for r in range(ext):
            at = r + PAD - STEPS
            wide_a[r, pl.ds(PAD + y, 64)] = jnp.broadcast_to(col_a[:, at : at + 1], (64, lanes))
            wide_b[r, pl.ds(y, 64)] = jnp.broadcast_to(col_b[:, at : at + 1], (64, lanes))

    def take(r, load):
        for y in range(0, ny, chunk):
            u[0, r, pl.ds(PAD + y, chunk)] = load(y).astype(jnp.float32)

    @pl.loop(0, rows)
    def _(r):
        take(r + STEPS, lambda y: f_ref[r, pl.ds(y, chunk)])

    @pl.when(tile > 0)
    def _():
        back.wait_send()
        ahead.wait_recv()

    @pl.when(tile < tiles - 1)
    def _():
        ahead.wait_send()
        back.wait_recv()

    @pl.when(tile == 0)
    def _():
        halo[0] = jnp.zeros((STEPS, ny, lanes), halo.dtype)

    @pl.when(tile == tiles - 1)
    def _():
        halo[1] = jnp.zeros((STEPS, ny, lanes), halo.dtype)

    @pl.loop(0, STEPS)
    def _(r):
        take(r, lambda y: halo[0, r, pl.ds(y, chunk)])
        take(r + STEPS + rows, lambda y: halo[1, r, pl.ds(y, chunk)])

    def stepped(src, r, y):
        at = pl.ds(PAD + y, chunk)
        sides = (r + 1, at), (r - 1, at), (r, pl.ds(PAD + y + 1, chunk)), (r, pl.ds(PAD + y - 1, chunk))
        coef = wide_a[r, at]
        value = wide_b[r, pl.ds(y, chunk)] * u[src, r, at]
        for i, j in sides:
            value = value + (coef + wide_a[i, j]) * u[src, i, j]
        return value

    def advance(step, low, high):
        def one(r, _):
            inside = ((r >= STEPS) | (tile > 0)) & ((r < STEPS + rows) | (tile < tiles - 1))
            mask = jnp.where(inside, 1.0, 0.0)
            for y in range(0, ny, chunk):
                u[step + 1, r, pl.ds(PAD + y, chunk)] = stepped(step, r, y) * mask
            return 0

        lax.fori_loop(low, high, one, 0)

    weight = jnp.sqrt(jnp.full((1, lanes), weight_ref[0].astype(jnp.float32)))
    copies = []
    for k in [k for k in range(cases) if k] + [0]:
        turn = lax.rem(case + k, cases)
        first = turn * quarter
        for step in range(STEPS - 1):
            reach = STEPS - 1 - step
            low = -reach if k == 1 else jnp.where(turn == 0, -reach, reach)
            advance(step, first + STEPS + low, first + STEPS + quarter + reach)

        @pl.loop(0, quarter)
        def _(i):
            for y in range(0, ny, chunk):
                value = (stepped(STEPS - 1, first + i + STEPS, y) * weight).astype(jnp.bfloat16)
                if k:
                    out[k, i, pl.ds(y, chunk)] = value
                else:
                    s_ref[case, i, pl.ds(y, chunk)] = value

        if k:
            copy = remote(out.at[k], s_ref.at[case], s_send.at[k], s_recv.at[k], case_peers[k])
            copy.start()
            copies.append(copy)
    for copy in copies:
        copy.wait()

    block = 0
    snaps = [s_ref[g].reshape(quarter * ny, lanes) for g in range(cases)]
    for g in range(cases):
        right = jnp.concatenate(snaps[g:], 1)
        terms = lax.dot_general(snaps[g], right, (((0,), (0,)), ((), ())), preferred_element_type=jnp.float32)
        for h in range(cases - g):
            flat[block * lanes : (block + 1) * lanes, :] = terms[:, h * lanes : (h + 1) * lanes]
            block += 1
    half, share = part.shape[2:4]
    for i in range(2 * cases * half):
        part[i // (cases * half), i // half % cases, i % half] = flat[i * share : (i + 1) * share, :]

    def exchange(devices, source, target, send, recv):
        started = [remote(source(k), target(k), send.at[k], recv.at[k], devices[k]) for k in range(1, len(devices))]
        for copy in started:
            copy.start()
        for copy in started:
            copy.wait()

    core, chip = lax.rem(tile, 2), lax.div(tile, 2)
    core_peers = [{"tile": tile}, {"tile": chip * 2 + 1 - core}]
    chip_peers = [{"tile": lax.rem(chip + k, half) * 2 + core} for k in range(half)]
    exchange(core_peers, lambda k: part.at[1 - core], lambda k: core_in, rs_send, rs_recv)
    core_sum[...] = part[core] + core_in[...]
    exchange(
        case_peers, lambda k: core_sum.at[lax.rem(case + k, cases)], lambda k: case_in.at[k], cs_send, cs_recv
    )
    total = core_sum[case]
    for k in range(1, cases):
        total = total + case_in[k]
    acc[...] = total
    exchange(
        chip_peers, lambda k: acc.at[lax.rem(chip + k, half)], lambda k: chip_in.at[k], ts_send, ts_recv
    )
    total = acc[chip]
    for k in range(1, half):
        total = total + chip_in[k]
    gram_ref[core, case, chip] = total
    mine = gram_ref.at[core, case, chip]
    exchange(chip_peers, lambda k: mine, lambda k: mine, tg_send, tg_recv)
    ours = gram_ref.at[core, case]
    exchange(case_peers, lambda k: ours, lambda k: ours, cg_send, cg_recv)
    exchange(core_peers, lambda k: gram_ref.at[core], lambda k: gram_ref.at[core], rg_send, rg_recv)


def front(cases, tiles, forcing, permeability, merge_weights):
    rows, ny, lanes = forcing.shape
    ext, quarter = rows + 2 * STEPS, rows // cases
    total = cases * (cases + 1) // 2 * lanes
    half = tiles // 2
    share = total // (2 * cases * half)
    f32, bf16 = jnp.float32, jnp.bfloat16
    vmem = pl.BlockSpec(memory_space=pltpu.VMEM)
    dma = pltpu.SemaphoreType.DMA
    return pl.pallas_call(
        functools.partial(front_kernel, cases, tiles),
        out_shape=(
            jax.ShapeDtypeStruct((cases, quarter, ny, lanes), bf16),
            jax.ShapeDtypeStruct((2, cases, half, share, lanes), f32),
        ),
        in_specs=[vmem, vmem, pl.BlockSpec(memory_space=pltpu.SMEM)],
        out_specs=(vmem, vmem),
        scratch_shapes=[
            pltpu.VMEM((2, STEPS, ny, lanes), bf16),
            pltpu.VMEM((lanes, ny), f32),
            pltpu.VMEM((ny + 2 * PAD, lanes), f32),
            pltpu.VMEM((STEPS, ext, ny + 2 * PAD, lanes), f32),
            pltpu.VMEM((ext, ny + 2 * PAD, lanes), f32),
            pltpu.VMEM((ext, ny, lanes), f32),
            pltpu.VMEM((cases, quarter, ny, lanes), bf16),
            pltpu.VMEM((total, lanes), f32),
            pltpu.VMEM((2, cases, half, share, lanes), f32),
            pltpu.VMEM((cases, half, share, lanes), f32),
            pltpu.VMEM((cases, half, share, lanes), f32),
            pltpu.VMEM((cases, half, share, lanes), f32),
            pltpu.VMEM((half, share, lanes), f32),
            pltpu.VMEM((half, share, lanes), f32),
            dma((2,)), dma((2,)),
            dma((2,)), dma((2,)),
            dma((cases,)), dma((cases,)),
            dma((2,)), dma((2,)),
            dma((cases,)), dma((cases,)),
            dma((half,)), dma((half,)),
            dma((half,)), dma((half,)),
            dma((cases,)), dma((cases,)),
            dma((2,)), dma((2,)),
        ],
        compiler_params=pltpu.CompilerParams(collective_id=0, has_side_effects=True, vmem_limit_bytes=VMEM_BYTES),
    )(forcing, permeability, merge_weights)


def dot(left, right):
    return jnp.dot(left, right, precision=HIGHEST, preferred_element_type=jnp.float32)


def dot_rows(left, right):
    return lax.dot_general(
        left, right, (((0,), (0,)), ((), ())), precision=HIGHEST, preferred_element_type=jnp.float32
    )


def inverse_factors(work, inners):
    count, size = len(inners), inners[0].shape[0]
    eye = (
        lax.broadcasted_iota(jnp.int32, (size, size), 0) == lax.broadcasted_iota(jnp.int32, (size, size), 1)
    ).astype(jnp.float32)
    for b in range(count):
        work[b, :, :size] = inners[b]
        work[b, :, size:] = eye
    shape = (count, PANEL, size)
    index = lax.broadcasted_iota(jnp.int32, shape, 1)
    for top in range(0, size, PANEL):
        left = work[:count, top : top + PANEL, :size]
        right = work[:count, top : top + PANEL, size:]
        scale = jnp.ones(shape, jnp.float32)
        for group in range(0, PANEL, GROUP):
            at = top + group
            columns = [jnp.broadcast_to(left[:, :, at + j : at + j + 1], shape) for j in range(GROUP)]
            for j in range(GROUP):
                i = group + j
                root = lax.rsqrt(columns[j][:, i : i + 1, :])
                scale = jnp.where(index == i, root, scale)
                factor = jnp.where(index > i, columns[j] * (root * root), 0.0)
                for m in range(j + 1, GROUP):
                    columns[m] = columns[m] - factor * columns[m][:, i : i + 1, :]
                left = left - factor * left[:, i : i + 1, :]
                right = right - factor * right[:, i : i + 1, :]
        panel = jnp.concatenate([left * scale, right * scale], 2)
        work[:count, top : top + PANEL, :] = panel
        below = top + PANEL
        if below < size:
            for b in range(count):
                lead = panel[b][:, :size]
                update = dot_rows(lead, panel[b])
                work[b, below:, :] = work[b, below:, :] - update[below:, :]
    return [work[b, :, size:] for b in range(count)]


def solve_kernel(cells, gram_ref, code_ref, out_ref, full, work):
    cases, lanes = out_ref.shape[0], out_ref.shape[2]
    case = lax.axis_index("case")
    block = 0
    for g in range(cases):
        for h in range(g, cases):
            value = gram_ref[block]
            full[g, h] = value
            if h != g:
                full[h, g] = value.T
            block += 1
    groups = [jnp.bitwise_xor(case, g) for g in range(cases)]
    grams = {(g, h): full[groups[g], groups[h]] for g in range(cases) for h in range(cases)}
    chains = [[0]]
    for level in range(LEVELS - 1, 0, -1):
        chains.insert(0, sorted({c ^ bit for c in chains[0] for bit in (0, 2**level)}))

    def joined(left, right):
        return jnp.concatenate([jnp.concatenate([grams[g, h] for h in right], 1) for g in left], 0)

    bases = {c: ([c], None) for c in range(cases)}
    for level in range(LEVELS):
        crossed = {}

        def cross(g, h):
            if (h, g) in crossed:
                return crossed[h, g].T
            if (g, h) not in crossed:
                value = dot(joined(bases[g][0], bases[h][0]), bases[h][1])
                crossed[g, h] = dot_rows(bases[g][1], value)
            return crossed[g, h]

        start = code_ref[level].astype(jnp.float32)
        coeffs, inners = [], []
        for c in chains[level]:
            pair = (c, c ^ 2**level)
            if level == 0:
                gram = joined(pair, pair)
            else:
                rows = []
                for g in pair:
                    parts = [cross(g, h) for h in pair]
                    rows.append(jnp.concatenate(parts, 1))
                gram = jnp.concatenate(rows, 0)
            first = dot(gram, start) / cells
            second = dot(gram, first) / cells
            coeff = second.astype(jnp.bfloat16).astype(jnp.float32)
            coeffs.append(coeff)
            inners.append(dot_rows(coeff, dot(gram, coeff)))
        inverses = inverse_factors(work, inners)
        updated = {}
        for i, c in enumerate(chains[level]):
            p = c ^ 2**level
            turned = lax.dot_general(
                coeffs[i], inverses[i], (((1,), (1,)), ((), ())), precision=HIGHEST, preferred_element_type=jnp.float32
            ) * math.sqrt(cells)
            if level == 0:
                updated[c] = ([c, p], turned)
            else:
                head, tail = turned[:lanes], turned[lanes:]
                updated[c] = (
                    bases[c][0] + bases[p][0],
                    jnp.concatenate([dot(bases[c][1], head), dot(bases[p][1], tail)], 0),
                )
        bases = updated
    members, matrix = bases[0]
    for i, g in enumerate(members):
        out_ref[groups[g]] = matrix[i * lanes : (i + 1) * lanes].astype(out_ref.dtype)


def solve(cases, cells, grams, codes):
    lanes = grams.shape[-1]
    vmem = pl.BlockSpec(memory_space=pltpu.VMEM)
    return pl.pallas_call(
        functools.partial(solve_kernel, cells),
        out_shape=jax.ShapeDtypeStruct((cases, lanes, lanes), jnp.bfloat16),
        in_specs=[vmem] * 2,
        out_specs=vmem,
        scratch_shapes=[
            pltpu.VMEM((cases, cases, lanes, lanes), jnp.float32),
            pltpu.VMEM((cases, lanes, 2 * lanes), jnp.float32),
        ],
        compiler_params=pltpu.CompilerParams(vmem_limit_bytes=VMEM_BYTES),
    )(grams, codes)


def back_kernel(cases, s_ref, m_ref, out_ref, buffer, m_in, send, recv, m_send, m_recv):
    case = lax.axis_index("case")
    case_peers = peers("case", cases)
    cells = s_ref.shape[1]
    pieces = send.shape[1]
    chunk = cells // pieces
    barrier(("case", cases))
    copies = [remote(m_ref, m_in.at[k], m_send.at[k], m_recv.at[k], case_peers[k]) for k in range(1, cases)]
    for copy in copies:
        copy.start()

    def product(i, matrix):
        at = pl.ds(i * chunk, chunk)
        left = jnp.concatenate([s_ref[g, at, :] for g in range(cases)], 1)
        return jnp.dot(left, matrix, preferred_element_type=jnp.float32).astype(out_ref.dtype)

    for i in range(pieces):
        out_ref[case, pl.ds(i * chunk, chunk), :] = product(i, m_ref[...])
    for copy in copies:
        copy.wait()
    copies = []
    for i in range(pieces):
        at = pl.ds(i * chunk, chunk)
        for k in range(1, cases):
            buffer[k, at, :] = product(i, m_in[cases - k])
            copy = remote(buffer.at[k, at], out_ref.at[case, at], send.at[k, i], recv.at[k, i], case_peers[k])
            copy.start()
            copies.append(copy)
    for copy in copies:
        copy.wait()


def back(cases, snaps, matrices):
    vmem = pl.BlockSpec(memory_space=pltpu.VMEM)
    return pl.pallas_call(
        functools.partial(back_kernel, cases),
        out_shape=jax.ShapeDtypeStruct(snaps.shape, jnp.bfloat16),
        in_specs=[vmem] * 2,
        out_specs=vmem,
        scratch_shapes=[
            pltpu.VMEM(snaps.shape, jnp.bfloat16),
            pltpu.VMEM((cases,) + matrices.shape, jnp.bfloat16),
            pltpu.SemaphoreType.DMA((cases, 4)),
            pltpu.SemaphoreType.DMA((cases, 4)),
            pltpu.SemaphoreType.DMA((cases,)),
            pltpu.SemaphoreType.DMA((cases,)),
        ],
        compiler_params=pltpu.CompilerParams(collective_id=1, has_side_effects=True, vmem_limit_bytes=VMEM_BYTES),
    )(snaps, matrices)


def per_device(cases, tiles, forcing, permeability, merge_weights, start_codes):
    _, rows, ny, lanes = forcing.shape
    snaps, grams = front(cases, tiles, forcing[0], permeability[0], merge_weights)
    cells = rows * tiles * ny
    matrices = solve(cases, cells, grams.reshape(-1, lanes, lanes), start_codes)
    basis = back(cases, snaps.reshape(cases, -1, lanes), matrices.reshape(-1, lanes))
    return basis.reshape(1, -1, lanes)


def solution(mesh):
    placed = (P("case", "tile", None, None), P("case", "tile", None), P("case"), P())
    return jax.shard_map(
        functools.partial(per_device, mesh.shape["case"], mesh.shape["tile"]),
        mesh=mesh, in_specs=placed, out_specs=P("case", "tile", None), check_vma=False,
    )
```

```python
import functools
import math

import jax
import jax.numpy as jnp
from jax import lax
from jax.experimental import pallas as pl
from jax.experimental.pallas import tpu as pltpu
from jax.sharding import PartitionSpec as P

STEPS = 3
LEVELS = 2
PAD = 8
PANEL = 16
GROUP = 8
HIGHEST = lax.Precision.HIGHEST
MESH = pl.DeviceIdType.MESH
VMEM_BYTES = 60 * 2**20


def peers(axis, size):
    me = lax.axis_index(axis)
    return [{axis: lax.rem(me + k, size)} for k in range(size)]


def barrier(*axes):
    sem = pltpu.get_barrier_semaphore()
    count = 0
    for axis, size in axes:
        for device in peers(axis, size)[1:]:
            pl.semaphore_signal(sem, inc=1, device_id=device, device_id_type=MESH)
            count += 1
    pl.semaphore_wait(sem, count)


def remote(src, dst, send, recv, device):
    return pltpu.make_async_remote_copy(
        src_ref=src, dst_ref=dst, send_sem=send, recv_sem=recv, device_id=device, device_id_type=MESH
    )


def front_kernel(
    cases, tiles, f_ref, p_ref, weight_ref, s_ref, gram_ref,
    halo, p_ext, p_turned, u, wide_a, wide_b, out, flat, part, core_in, core_sum, case_in, acc, chip_in,
    halo_send, halo_recv, p_send, p_recv, s_send, s_recv,
    rs_send, rs_recv, cs_send, cs_recv, ts_send, ts_recv, tg_send, tg_recv, cg_send, cg_recv, rg_send, rg_recv,
):
    rows, ny, lanes = f_ref.shape
    ext = rows + 2 * STEPS
    quarter = rows // cases
    case, tile = lax.axis_index("case"), lax.axis_index("tile")
    case_peers, tile_peers = peers("case", cases), peers("tile", tiles)
    chunk = 128
    barrier(("case", cases), ("tile", tiles))

    back = remote(f_ref.at[pl.ds(0, STEPS)], halo.at[1], halo_send.at[0], halo_recv.at[1], {"tile": tile - 1})
    ahead = remote(f_ref.at[pl.ds(rows - STEPS, STEPS)], halo.at[0], halo_send.at[1], halo_recv.at[0], {"tile": tile + 1})

    p_back = remote(
        p_ref.at[pl.ds(0, PAD)], p_ext.at[pl.ds(PAD + rows, PAD)], p_send.at[0], p_recv.at[1], {"tile": tile - 1}
    )
    p_ahead = remote(
        p_ref.at[pl.ds(rows - PAD, PAD)], p_ext.at[pl.ds(0, PAD)], p_send.at[1], p_recv.at[0], {"tile": tile + 1}
    )

    @pl.when(tile > 0)
    def _():
        p_back.start()
        back.start()

    @pl.when(tile < tiles - 1)
    def _():
        p_ahead.start()
        ahead.start()

    @pl.when(tile == 0)
    def _():
        p_ext[0:PAD] = jnp.zeros((PAD, ny), jnp.float32)

    @pl.when(tile == tiles - 1)
    def _():
        p_ext[PAD + rows : 2 * PAD + rows] = jnp.zeros((PAD, ny), jnp.float32)

    p_ext[PAD : PAD + rows] = p_ref[...]
    p_ext[2 * PAD + rows :] = jnp.zeros((lanes - 2 * PAD - rows, ny), jnp.float32)
    p_turned[0:PAD] = jnp.zeros((PAD, lanes), jnp.float32)
    p_turned[PAD + ny :] = jnp.zeros((PAD, lanes), jnp.float32)

    @pl.loop(0, ext)
    def _(r):
        zeros = jnp.zeros((PAD, lanes), jnp.float32)
        for at in (pl.ds(0, PAD), pl.ds(PAD + ny, PAD)):
            wide_a[r, at] = zeros
            for slot in range(STEPS):
                u[slot, r, at] = zeros

    @pl.when(tile > 0)
    def _():
        p_back.wait_send()
        p_ahead.wait_recv()

    @pl.when(tile < tiles - 1)
    def _():
        p_ahead.wait_send()
        p_back.wait_recv()

    for y in range(0, ny, lanes):
        p_turned[pl.ds(PAD + y, lanes)] = p_ext[:, y : y + lanes].T
    for y in range(0, ny, 64):
        mid = p_turned[pl.ds(PAD + y, 64)]
        around = p_turned[pl.ds(PAD + y + 1, 64)] + p_turned[pl.ds(PAD + y - 1, 64)]
        around = around + (pltpu.roll(mid, 1, 1) + pltpu.roll(mid, lanes - 1, 1))
        col_a = 0.12 * mid
        col_b = 1.0 - 0.12 * (4.0 * mid + around)
        for r in range(ext):
            at = r + PAD - STEPS
            wide_a[r, pl.ds(PAD + y, 64)] = jnp.broadcast_to(col_a[:, at : at + 1], (64, lanes))
            wide_b[r, pl.ds(y, 64)] = jnp.broadcast_to(col_b[:, at : at + 1], (64, lanes))

    def take(r, load):
        for y in range(0, ny, chunk):
            u[0, r, pl.ds(PAD + y, chunk)] = load(y).astype(jnp.float32)

    @pl.loop(0, rows)
    def _(r):
        take(r + STEPS, lambda y: f_ref[r, pl.ds(y, chunk)])

    @pl.when(tile > 0)
    def _():
        back.wait_send()
        ahead.wait_recv()

    @pl.when(tile < tiles - 1)
    def _():
        ahead.wait_send()
        back.wait_recv()

    @pl.when(tile == 0)
    def _():
        halo[0] = jnp.zeros((STEPS, ny, lanes), halo.dtype)

    @pl.when(tile == tiles - 1)
    def _():
        halo[1] = jnp.zeros((STEPS, ny, lanes), halo.dtype)

    @pl.loop(0, STEPS)
    def _(r):
        take(r, lambda y: halo[0, r, pl.ds(y, chunk)])
        take(r + STEPS + rows, lambda y: halo[1, r, pl.ds(y, chunk)])

    def stepped(src, r, y):
        at = pl.ds(PAD + y, chunk)
        sides = (r + 1, at), (r - 1, at), (r, pl.ds(PAD + y + 1, chunk)), (r, pl.ds(PAD + y - 1, chunk))
        coef = wide_a[r, at]
        value = wide_b[r, pl.ds(y, chunk)] * u[src, r, at]
        for i, j in sides:
            value = value + (coef + wide_a[i, j]) * u[src, i, j]
        return value

    def advance(step, low, high):
        def one(r, _):
            inside = ((r >= STEPS) | (tile > 0)) & ((r < STEPS + rows) | (tile < tiles - 1))
            mask = jnp.where(inside, 1.0, 0.0)
            for y in range(0, ny, chunk):
                u[step + 1, r, pl.ds(PAD + y, chunk)] = stepped(step, r, y) * mask
            return 0

        lax.fori_loop(low, high, one, 0)

    weight = jnp.sqrt(jnp.full((1, lanes), weight_ref[0].astype(jnp.float32)))
    def row_copy(k, i):
        return remote(out.at[k, i], s_ref.at[case, i], s_send.at[k, i], s_recv.at[k, i], case_peers[k])

    for k in [k for k in range(cases) if k] + [0]:
        turn = lax.rem(case + k, cases)
        first = turn * quarter
        for step in range(STEPS - 1):
            reach = STEPS - 1 - step
            low = -reach if k == 1 else jnp.where(turn == 0, -reach, reach)
            advance(step, first + STEPS + low, first + STEPS + quarter + reach)

        @pl.loop(0, quarter)
        def _(i):
            for y in range(0, ny, chunk):
                value = (stepped(STEPS - 1, first + i + STEPS, y) * weight).astype(jnp.bfloat16)
                if k:
                    out[k, i, pl.ds(y, chunk)] = value
                else:
                    s_ref[case, i, pl.ds(y, chunk)] = value

            if k:
                row_copy(k, i).start()

    for i in range(quarter):
        for k in range(1, cases):
            row_copy(k, i).wait()

    block = 0
    snaps = [s_ref[g].reshape(quarter * ny, lanes) for g in range(cases)]
    for g in range(cases):
        right = jnp.concatenate(snaps[g:], 1)
        terms = lax.dot_general(snaps[g], right, (((0,), (0,)), ((), ())), preferred_element_type=jnp.float32)
        for h in range(cases - g):
            flat[block * lanes : (block + 1) * lanes, :] = terms[:, h * lanes : (h + 1) * lanes]
            block += 1
    half, share = part.shape[2:4]
    for i in range(2 * cases * half):
        part[i // (cases * half), i // half % cases, i % half] = flat[i * share : (i + 1) * share, :]

    def exchange(devices, source, target, send, recv):
        started = [remote(source(k), target(k), send.at[k], recv.at[k], devices[k]) for k in range(1, len(devices))]
        for copy in started:
            copy.start()
        for copy in started:
            copy.wait()

    core, chip = lax.rem(tile, 2), lax.div(tile, 2)
    core_peers = [{"tile": tile}, {"tile": chip * 2 + 1 - core}]
    chip_peers = [{"tile": lax.rem(chip + k, half) * 2 + core} for k in range(half)]
    exchange(core_peers, lambda k: part.at[1 - core], lambda k: core_in, rs_send, rs_recv)
    core_sum[...] = part[core] + core_in[...]
    exchange(
        case_peers, lambda k: core_sum.at[lax.rem(case + k, cases)], lambda k: case_in.at[k], cs_send, cs_recv
    )
    total = core_sum[case]
    for k in range(1, cases):
        total = total + case_in[k]
    acc[...] = total
    exchange(
        chip_peers, lambda k: acc.at[lax.rem(chip + k, half)], lambda k: chip_in.at[k], ts_send, ts_recv
    )
    total = acc[chip]
    for k in range(1, half):
        total = total + chip_in[k]
    gram_ref[core, case, chip] = total
    mine = gram_ref.at[core, case, chip]
    exchange(chip_peers, lambda k: mine, lambda k: mine, tg_send, tg_recv)
    ours = gram_ref.at[core, case]
    exchange(case_peers, lambda k: ours, lambda k: ours, cg_send, cg_recv)
    exchange(core_peers, lambda k: gram_ref.at[core], lambda k: gram_ref.at[core], rg_send, rg_recv)


def front(cases, tiles, forcing, permeability, merge_weights):
    rows, ny, lanes = forcing.shape
    ext, quarter = rows + 2 * STEPS, rows // cases
    total = cases * (cases + 1) // 2 * lanes
    half = tiles // 2
    share = total // (2 * cases * half)
    f32, bf16 = jnp.float32, jnp.bfloat16
    vmem = pl.BlockSpec(memory_space=pltpu.VMEM)
    dma = pltpu.SemaphoreType.DMA
    return pl.pallas_call(
        functools.partial(front_kernel, cases, tiles),
        out_shape=(
            jax.ShapeDtypeStruct((cases, quarter, ny, lanes), bf16),
            jax.ShapeDtypeStruct((2, cases, half, share, lanes), f32),
        ),
        in_specs=[vmem, vmem, pl.BlockSpec(memory_space=pltpu.SMEM)],
        out_specs=(vmem, vmem),
        scratch_shapes=[
            pltpu.VMEM((2, STEPS, ny, lanes), bf16),
            pltpu.VMEM((lanes, ny), f32),
            pltpu.VMEM((ny + 2 * PAD, lanes), f32),
            pltpu.VMEM((STEPS, ext, ny + 2 * PAD, lanes), f32),
            pltpu.VMEM((ext, ny + 2 * PAD, lanes), f32),
            pltpu.VMEM((ext, ny, lanes), f32),
            pltpu.VMEM((cases, quarter, ny, lanes), bf16),
            pltpu.VMEM((total, lanes), f32),
            pltpu.VMEM((2, cases, half, share, lanes), f32),
            pltpu.VMEM((cases, half, share, lanes), f32),
            pltpu.VMEM((cases, half, share, lanes), f32),
            pltpu.VMEM((cases, half, share, lanes), f32),
            pltpu.VMEM((half, share, lanes), f32),
            pltpu.VMEM((half, share, lanes), f32),
            dma((2,)), dma((2,)),
            dma((2,)), dma((2,)),
            dma((cases, quarter)), dma((cases, quarter)),
            dma((2,)), dma((2,)),
            dma((cases,)), dma((cases,)),
            dma((half,)), dma((half,)),
            dma((half,)), dma((half,)),
            dma((cases,)), dma((cases,)),
            dma((2,)), dma((2,)),
        ],
        compiler_params=pltpu.CompilerParams(collective_id=0, has_side_effects=True, vmem_limit_bytes=VMEM_BYTES),
    )(forcing, permeability, merge_weights)


def dot(left, right):
    return jnp.dot(left, right, precision=HIGHEST, preferred_element_type=jnp.float32)


def dot_rows(left, right):
    return lax.dot_general(
        left, right, (((0,), (0,)), ((), ())), precision=HIGHEST, preferred_element_type=jnp.float32
    )


def inverse_factors(work, inners):
    count, size = len(inners), inners[0].shape[0]
    eye = (
        lax.broadcasted_iota(jnp.int32, (size, size), 0) == lax.broadcasted_iota(jnp.int32, (size, size), 1)
    ).astype(jnp.float32)
    for b in range(count):
        work[b, :, :size] = inners[b]
        work[b, :, size:] = eye
    shape = (count, PANEL, size)
    index = lax.broadcasted_iota(jnp.int32, shape, 1)
    for top in range(0, size, PANEL):
        left = work[:count, top : top + PANEL, :size]
        right = work[:count, top : top + PANEL, size:]
        scale = jnp.ones(shape, jnp.float32)
        for group in range(0, PANEL, GROUP):
            at = top + group
            columns = [jnp.broadcast_to(left[:, :, at + j : at + j + 1], shape) for j in range(GROUP)]
            for j in range(GROUP):
                i = group + j
                root = lax.rsqrt(columns[j][:, i : i + 1, :])
                scale = jnp.where(index == i, root, scale)
                factor = jnp.where(index > i, columns[j] * (root * root), 0.0)
                for m in range(j + 1, GROUP):
                    columns[m] = columns[m] - factor * columns[m][:, i : i + 1, :]
                left = left - factor * left[:, i : i + 1, :]
                right = right - factor * right[:, i : i + 1, :]
        panel = jnp.concatenate([left * scale, right * scale], 2)
        work[:count, top : top + PANEL, :] = panel
        below = top + PANEL
        if below < size:
            for b in range(count):
                lead = panel[b][:, :size]
                update = dot_rows(lead, panel[b])
                work[b, below:, :] = work[b, below:, :] - update[below:, :]
    return [work[b, :, size:] for b in range(count)]


def solve_kernel(cells, gram_ref, code_ref, out_ref, full, work):
    cases, lanes = out_ref.shape[1:3]
    case = lax.axis_index("case")
    block = 0
    for g in range(cases):
        for h in range(g, cases):
            value = gram_ref[block]
            full[g, h] = value
            if h != g:
                full[h, g] = value.T
            block += 1
    groups = [jnp.bitwise_xor(case, g) for g in range(cases)]
    grams = {(g, h): full[groups[g], groups[h]] for g in range(cases) for h in range(cases)}
    chains = [[0, 2 ** (LEVELS - 1)]]
    for level in range(LEVELS - 1, 0, -1):
        chains.insert(0, sorted({c ^ bit for c in chains[0] for bit in (0, 2**level)}))

    def joined(left, right):
        return jnp.concatenate([jnp.concatenate([grams[g, h] for h in right], 1) for g in left], 0)

    bases = {c: ([c], None) for c in range(cases)}
    for level in range(LEVELS):
        crossed = {}

        def cross(g, h):
            if (h, g) in crossed:
                return crossed[h, g].T
            if (g, h) not in crossed:
                value = dot(joined(bases[g][0], bases[h][0]), bases[h][1])
                crossed[g, h] = dot_rows(bases[g][1], value)
            return crossed[g, h]

        start = code_ref[level].astype(jnp.float32)
        coeffs, inners = [], []
        for c in chains[level]:
            pair = (c, c ^ 2**level)
            if level == 0:
                gram = joined(pair, pair)
            else:
                rows = []
                for g in pair:
                    parts = [cross(g, h) for h in pair]
                    rows.append(jnp.concatenate(parts, 1))
                gram = jnp.concatenate(rows, 0)
            first = dot(gram, start) / cells
            second = dot(gram, first) / cells
            coeff = second.astype(jnp.bfloat16).astype(jnp.float32)
            coeffs.append(coeff)
            inners.append(dot_rows(coeff, dot(gram, coeff)))
        inverses = inverse_factors(work, inners)
        updated = {}
        for i, c in enumerate(chains[level]):
            p = c ^ 2**level
            turned = lax.dot_general(
                coeffs[i], inverses[i], (((1,), (1,)), ((), ())), precision=HIGHEST, preferred_element_type=jnp.float32
            ) * math.sqrt(cells)
            if level == 0:
                updated[c] = ([c, p], turned)
            else:
                head, tail = turned[:lanes], turned[lanes:]
                updated[c] = (
                    bases[c][0] + bases[p][0],
                    jnp.concatenate([dot(bases[c][1], head), dot(bases[p][1], tail)], 0),
                )
        bases = updated
    for slot, c in enumerate(chains[-1]):
        members, matrix = bases[c]
        for i, g in enumerate(members):
            out_ref[slot, groups[g]] = matrix[i * lanes : (i + 1) * lanes].astype(out_ref.dtype)


def solve(cases, cells, grams, codes):
    lanes = grams.shape[-1]
    vmem = pl.BlockSpec(memory_space=pltpu.VMEM)
    return pl.pallas_call(
        functools.partial(solve_kernel, cells),
        out_shape=jax.ShapeDtypeStruct((2, cases, lanes, lanes), jnp.bfloat16),
        in_specs=[vmem] * 2,
        out_specs=vmem,
        scratch_shapes=[
            pltpu.VMEM((cases, cases, lanes, lanes), jnp.float32),
            pltpu.VMEM((cases, lanes, 2 * lanes), jnp.float32),
        ],
        compiler_params=pltpu.CompilerParams(vmem_limit_bytes=VMEM_BYTES),
    )(grams, codes)


def back_kernel(cases, s_ref, m_ref, out_ref, buffer, m_in, send, recv, m_send, m_recv):
    case, tile = lax.axis_index("case"), lax.axis_index("tile")
    core = lax.rem(tile, 2)
    cells = s_ref.shape[1]
    pieces = send.shape[1]
    chunk = cells // pieces
    beside = case + 1 - 2 * lax.rem(case, 2)
    devices = [{"case": lax.rem(case + cases // 2, cases)}, {"case": beside}, {"case": lax.rem(beside + cases // 2, cases)}]
    twin = {"tile": tile + 1 - 2 * core}
    sem = pltpu.get_barrier_semaphore()
    for device in devices + [twin]:
        pl.semaphore_signal(sem, inc=1, device_id=device, device_id_type=MESH)
    pl.semaphore_wait(sem, len(devices) + 1)

    depth = m_ref.shape[1] // 2
    part = pl.ds(pl.multiple_of(core * depth, depth), depth)
    across = remote(m_ref.at[:, part], m_in.at[:, part], m_send.at[0], m_recv.at[0], devices[1])
    swap = remote(m_in.at[:, part], m_in.at[:, part], m_send.at[1], m_recv.at[1], twin)
    across.start()

    def product(i, matrix):
        left = jnp.concatenate([s_ref[g, pl.ds(i * chunk, chunk), :] for g in range(cases)], 1)
        return jnp.dot(left, matrix, preferred_element_type=jnp.float32).astype(out_ref.dtype)

    copies = []

    def deliver(i, k, matrix):
        at = pl.ds(i * chunk, chunk)
        buffer[k, at, :] = product(i, matrix)
        copy = remote(buffer.at[k, at], out_ref.at[case, at], send.at[k, i], recv.at[k, i], devices[k])
        copy.start()
        copies.append(copy)

    for i in range(pieces):
        deliver(i, 0, m_ref[1])
    across.wait()
    swap.start()
    for i in range(pieces):
        out_ref[case, pl.ds(i * chunk, chunk), :] = product(i, m_ref[0])
    swap.wait()
    for i in range(pieces):
        for k in (1, 2):
            deliver(i, k, m_in[k - 1])
    for copy in copies:
        copy.wait()


def back(cases, snaps, matrices):
    vmem = pl.BlockSpec(memory_space=pltpu.VMEM)
    return pl.pallas_call(
        functools.partial(back_kernel, cases),
        out_shape=jax.ShapeDtypeStruct(snaps.shape, jnp.bfloat16),
        in_specs=[vmem] * 2,
        out_specs=vmem,
        scratch_shapes=[
            pltpu.VMEM(snaps.shape, jnp.bfloat16),
            pltpu.VMEM(matrices.shape, jnp.bfloat16),
            pltpu.SemaphoreType.DMA((cases, 4)),
            pltpu.SemaphoreType.DMA((cases, 4)),
            pltpu.SemaphoreType.DMA((2,)),
            pltpu.SemaphoreType.DMA((2,)),
        ],
        compiler_params=pltpu.CompilerParams(collective_id=1, has_side_effects=True, vmem_limit_bytes=VMEM_BYTES),
    )(snaps, matrices)


def per_device(cases, tiles, forcing, permeability, merge_weights, start_codes):
    _, rows, ny, lanes = forcing.shape
    snaps, grams = front(cases, tiles, forcing[0], permeability[0], merge_weights)
    cells = rows * tiles * ny
    matrices = solve(cases, cells, grams.reshape(-1, lanes, lanes), start_codes)
    basis = back(cases, snaps.reshape(cases, -1, lanes), matrices.reshape(2, -1, lanes))
    return basis.reshape(1, -1, lanes)


def solution(mesh):
    placed = (P("case", "tile", None, None), P("case", "tile", None), P("case"), P())
    return jax.shard_map(
        functools.partial(per_device, mesh.shape["case"], mesh.shape["tile"]),
        mesh=mesh, in_specs=placed, out_specs=P("case", "tile", None), check_vma=False,
    )
```

```python
import functools
import math

import jax
import jax.numpy as jnp
from jax import lax
from jax.experimental import pallas as pl
from jax.experimental.pallas import tpu as pltpu
from jax.sharding import PartitionSpec as P

STEPS = 3
LEVELS = 2
PAD = 8
PANEL = 32
GROUP = 8
HIGHEST = lax.Precision.HIGHEST
MESH = pl.DeviceIdType.MESH
VMEM_BYTES = 60 * 2**20


def peers(axis, size):
    me = lax.axis_index(axis)
    return [{axis: lax.rem(me + k, size)} for k in range(size)]


def barrier(*axes):
    sem = pltpu.get_barrier_semaphore()
    count = 0
    for axis, size in axes:
        for device in peers(axis, size)[1:]:
            pl.semaphore_signal(sem, inc=1, device_id=device, device_id_type=MESH)
            count += 1
    pl.semaphore_wait(sem, count)


def remote(src, dst, send, recv, device):
    return pltpu.make_async_remote_copy(
        src_ref=src, dst_ref=dst, send_sem=send, recv_sem=recv, device_id=device, device_id_type=MESH
    )


def front_kernel(
    cases, tiles, f_ref, p_ref, weight_ref, s_ref, gram_ref,
    halo, p_ext, p_turned, u, wide_a, wide_b, out, flat, part, core_in, core_sum, case_in, acc, chip_in,
    halo_send, halo_recv, p_send, p_recv, s_send, s_recv,
    rs_send, rs_recv, cs_send, cs_recv, ts_send, ts_recv, tg_send, tg_recv, cg_send, cg_recv, rg_send, rg_recv,
):
    rows, ny, lanes = f_ref.shape
    ext = rows + 2 * STEPS
    quarter = rows // cases
    case, tile = lax.axis_index("case"), lax.axis_index("tile")
    case_peers, tile_peers = peers("case", cases), peers("tile", tiles)
    chunk = 128
    barrier(("case", cases), ("tile", tiles))

    back = remote(f_ref.at[pl.ds(0, STEPS)], halo.at[1], halo_send.at[0], halo_recv.at[1], {"tile": tile - 1})
    ahead = remote(f_ref.at[pl.ds(rows - STEPS, STEPS)], halo.at[0], halo_send.at[1], halo_recv.at[0], {"tile": tile + 1})

    p_back = remote(
        p_ref.at[pl.ds(0, PAD)], p_ext.at[pl.ds(PAD + rows, PAD)], p_send.at[0], p_recv.at[1], {"tile": tile - 1}
    )
    p_ahead = remote(
        p_ref.at[pl.ds(rows - PAD, PAD)], p_ext.at[pl.ds(0, PAD)], p_send.at[1], p_recv.at[0], {"tile": tile + 1}
    )

    @pl.when(tile > 0)
    def _():
        p_back.start()
        back.start()

    @pl.when(tile < tiles - 1)
    def _():
        p_ahead.start()
        ahead.start()

    @pl.when(tile == 0)
    def _():
        p_ext[0:PAD] = jnp.zeros((PAD, ny), jnp.float32)

    @pl.when(tile == tiles - 1)
    def _():
        p_ext[PAD + rows : 2 * PAD + rows] = jnp.zeros((PAD, ny), jnp.float32)

    p_ext[PAD : PAD + rows] = p_ref[...]
    p_ext[2 * PAD + rows :] = jnp.zeros((lanes - 2 * PAD - rows, ny), jnp.float32)
    p_turned[0:PAD] = jnp.zeros((PAD, lanes), jnp.float32)
    p_turned[PAD + ny :] = jnp.zeros((PAD, lanes), jnp.float32)

    @pl.loop(0, ext)
    def _(r):
        zeros = jnp.zeros((PAD, lanes), jnp.float32)
        for at in (pl.ds(0, PAD), pl.ds(PAD + ny, PAD)):
            wide_a[r, at] = zeros
            for slot in range(STEPS):
                u[slot, r, at] = zeros

    @pl.when(tile > 0)
    def _():
        p_back.wait_send()
        p_ahead.wait_recv()

    @pl.when(tile < tiles - 1)
    def _():
        p_ahead.wait_send()
        p_back.wait_recv()

    for y in range(0, ny, lanes):
        p_turned[pl.ds(PAD + y, lanes)] = p_ext[:, y : y + lanes].T
    for y in range(0, ny, 64):
        mid = p_turned[pl.ds(PAD + y, 64)]
        around = p_turned[pl.ds(PAD + y + 1, 64)] + p_turned[pl.ds(PAD + y - 1, 64)]
        around = around + (pltpu.roll(mid, 1, 1) + pltpu.roll(mid, lanes - 1, 1))
        col_a = 0.12 * mid
        col_b = 1.0 - 0.12 * (4.0 * mid + around)
        for r in range(ext):
            at = r + PAD - STEPS
            wide_a[r, pl.ds(PAD + y, 64)] = jnp.broadcast_to(col_a[:, at : at + 1], (64, lanes))
            wide_b[r, pl.ds(y, 64)] = jnp.broadcast_to(col_b[:, at : at + 1], (64, lanes))

    def take(r, load):
        for y in range(0, ny, chunk):
            u[0, r, pl.ds(PAD + y, chunk)] = load(y).astype(jnp.float32)

    @pl.loop(0, rows)
    def _(r):
        take(r + STEPS, lambda y: f_ref[r, pl.ds(y, chunk)])

    @pl.when(tile > 0)
    def _():
        back.wait_send()
        ahead.wait_recv()

    @pl.when(tile < tiles - 1)
    def _():
        ahead.wait_send()
        back.wait_recv()

    @pl.when(tile == 0)
    def _():
        halo[0] = jnp.zeros((STEPS, ny, lanes), halo.dtype)

    @pl.when(tile == tiles - 1)
    def _():
        halo[1] = jnp.zeros((STEPS, ny, lanes), halo.dtype)

    @pl.loop(0, STEPS)
    def _(r):
        take(r, lambda y: halo[0, r, pl.ds(y, chunk)])
        take(r + STEPS + rows, lambda y: halo[1, r, pl.ds(y, chunk)])

    def stepped(src, r, y):
        at = pl.ds(PAD + y, chunk)
        sides = (r + 1, at), (r - 1, at), (r, pl.ds(PAD + y + 1, chunk)), (r, pl.ds(PAD + y - 1, chunk))
        coef = wide_a[r, at]
        value = wide_b[r, pl.ds(y, chunk)] * u[src, r, at]
        for i, j in sides:
            value = value + (coef + wide_a[i, j]) * u[src, i, j]
        return value

    def advance(step, low, high):
        def one(r, _):
            inside = ((r >= STEPS) | (tile > 0)) & ((r < STEPS + rows) | (tile < tiles - 1))
            mask = jnp.where(inside, 1.0, 0.0)
            for y in range(0, ny, chunk):
                u[step + 1, r, pl.ds(PAD + y, chunk)] = stepped(step, r, y) * mask
            return 0

        lax.fori_loop(low, high, one, 0)

    weight = jnp.sqrt(jnp.full((1, lanes), weight_ref[0].astype(jnp.float32)))
    def row_copy(k, i):
        return remote(out.at[k, i], s_ref.at[case, i], s_send.at[k, i], s_recv.at[k, i], case_peers[k])

    for k in [k for k in range(cases) if k] + [0]:
        turn = lax.rem(case + k, cases)
        first = turn * quarter
        for step in range(STEPS - 1):
            reach = STEPS - 1 - step
            low = -reach if k == 1 else jnp.where(turn == 0, -reach, reach)
            advance(step, first + STEPS + low, first + STEPS + quarter + reach)

        @pl.loop(0, quarter)
        def _(i):
            for y in range(0, ny, chunk):
                value = (stepped(STEPS - 1, first + i + STEPS, y) * weight).astype(jnp.bfloat16)
                if k:
                    out[k, i, pl.ds(y, chunk)] = value
                else:
                    s_ref[case, i, pl.ds(y, chunk)] = value

            if k:
                row_copy(k, i).start()

    for i in range(quarter):
        for k in range(1, cases):
            row_copy(k, i).wait()

    block = 0
    snaps = [s_ref[g].reshape(quarter * ny, lanes) for g in range(cases)]
    for g in range(cases):
        right = jnp.concatenate(snaps[g:], 1)
        terms = lax.dot_general(snaps[g], right, (((0,), (0,)), ((), ())), preferred_element_type=jnp.float32)
        for h in range(cases - g):
            flat[block * lanes : (block + 1) * lanes, :] = terms[:, h * lanes : (h + 1) * lanes]
            block += 1
    half, share = part.shape[2:4]
    for i in range(2 * cases * half):
        part[i // (cases * half), i // half % cases, i % half] = flat[i * share : (i + 1) * share, :]

    def exchange(devices, source, target, send, recv):
        started = [remote(source(k), target(k), send.at[k], recv.at[k], devices[k]) for k in range(1, len(devices))]
        for copy in started:
            copy.start()
        for copy in started:
            copy.wait()

    core, chip = lax.rem(tile, 2), lax.div(tile, 2)
    core_peers = [{"tile": tile}, {"tile": chip * 2 + 1 - core}]
    chip_peers = [{"tile": lax.rem(chip + k, half) * 2 + core} for k in range(half)]
    exchange(core_peers, lambda k: part.at[1 - core], lambda k: core_in, rs_send, rs_recv)
    core_sum[...] = part[core] + core_in[...]
    exchange(
        case_peers, lambda k: core_sum.at[lax.rem(case + k, cases)], lambda k: case_in.at[k], cs_send, cs_recv
    )
    total = core_sum[case]
    for k in range(1, cases):
        total = total + case_in[k]
    acc[...] = total
    exchange(
        chip_peers, lambda k: acc.at[lax.rem(chip + k, half)], lambda k: chip_in.at[k], ts_send, ts_recv
    )
    total = acc[chip]
    for k in range(1, half):
        total = total + chip_in[k]
    gram_ref[core, case, chip] = total
    mine = gram_ref.at[core, case, chip]
    exchange(chip_peers, lambda k: mine, lambda k: mine, tg_send, tg_recv)
    ours = gram_ref.at[core, case]
    exchange(case_peers, lambda k: ours, lambda k: ours, cg_send, cg_recv)
    exchange(core_peers, lambda k: gram_ref.at[core], lambda k: gram_ref.at[core], rg_send, rg_recv)


def front(cases, tiles, forcing, permeability, merge_weights):
    rows, ny, lanes = forcing.shape
    ext, quarter = rows + 2 * STEPS, rows // cases
    total = cases * (cases + 1) // 2 * lanes
    half = tiles // 2
    share = total // (2 * cases * half)
    f32, bf16 = jnp.float32, jnp.bfloat16
    vmem = pl.BlockSpec(memory_space=pltpu.VMEM)
    dma = pltpu.SemaphoreType.DMA
    return pl.pallas_call(
        functools.partial(front_kernel, cases, tiles),
        out_shape=(
            jax.ShapeDtypeStruct((cases, quarter, ny, lanes), bf16),
            jax.ShapeDtypeStruct((2, cases, half, share, lanes), f32),
        ),
        in_specs=[vmem, vmem, pl.BlockSpec(memory_space=pltpu.SMEM)],
        out_specs=(vmem, vmem),
        scratch_shapes=[
            pltpu.VMEM((2, STEPS, ny, lanes), bf16),
            pltpu.VMEM((lanes, ny), f32),
            pltpu.VMEM((ny + 2 * PAD, lanes), f32),
            pltpu.VMEM((STEPS, ext, ny + 2 * PAD, lanes), f32),
            pltpu.VMEM((ext, ny + 2 * PAD, lanes), f32),
            pltpu.VMEM((ext, ny, lanes), f32),
            pltpu.VMEM((cases, quarter, ny, lanes), bf16),
            pltpu.VMEM((total, lanes), f32),
            pltpu.VMEM((2, cases, half, share, lanes), f32),
            pltpu.VMEM((cases, half, share, lanes), f32),
            pltpu.VMEM((cases, half, share, lanes), f32),
            pltpu.VMEM((cases, half, share, lanes), f32),
            pltpu.VMEM((half, share, lanes), f32),
            pltpu.VMEM((half, share, lanes), f32),
            dma((2,)), dma((2,)),
            dma((2,)), dma((2,)),
            dma((cases, quarter)), dma((cases, quarter)),
            dma((2,)), dma((2,)),
            dma((cases,)), dma((cases,)),
            dma((half,)), dma((half,)),
            dma((half,)), dma((half,)),
            dma((cases,)), dma((cases,)),
            dma((2,)), dma((2,)),
        ],
        compiler_params=pltpu.CompilerParams(collective_id=0, has_side_effects=True, vmem_limit_bytes=VMEM_BYTES),
    )(forcing, permeability, merge_weights)


def dot(left, right):
    return jnp.dot(left, right, precision=HIGHEST, preferred_element_type=jnp.float32)


def dot_rows(left, right):
    return lax.dot_general(
        left, right, (((0,), (0,)), ((), ())), precision=HIGHEST, preferred_element_type=jnp.float32
    )


def inverse_factors(work, inners):
    count, size = len(inners), inners[0].shape[0]
    eye = (
        lax.broadcasted_iota(jnp.int32, (size, size), 0) == lax.broadcasted_iota(jnp.int32, (size, size), 1)
    ).astype(jnp.float32)
    for b in range(count):
        work[b, :, :size] = inners[b]
        work[b, :, size:] = eye
    shape = (count, PANEL, size)
    index = lax.broadcasted_iota(jnp.int32, shape, 1)
    for top in range(0, size, PANEL):
        left = work[:count, top : top + PANEL, :size]
        right = work[:count, top : top + PANEL, size:]
        scale = jnp.ones(shape, jnp.float32)
        for group in range(0, PANEL, GROUP):
            at = top + group
            columns = [jnp.broadcast_to(left[:, :, at + j : at + j + 1], shape) for j in range(GROUP)]
            for j in range(GROUP):
                i = group + j
                root = lax.rsqrt(columns[j][:, i : i + 1, :])
                scale = jnp.where(index == i, root, scale)
                factor = jnp.where(index > i, columns[j] * (root * root), 0.0)
                for m in range(j + 1, GROUP):
                    columns[m] = columns[m] - factor * columns[m][:, i : i + 1, :]
                left = left - factor * left[:, i : i + 1, :]
                right = right - factor * right[:, i : i + 1, :]
        panel = jnp.concatenate([left * scale, right * scale], 2)
        work[:count, top : top + PANEL, :] = panel
        below = top + PANEL
        if below < size:
            for b in range(count):
                lead = panel[b][:, :size]
                update = dot_rows(lead, panel[b])
                work[b, below:, :] = work[b, below:, :] - update[below:, :]
    return [work[b, :, size:] for b in range(count)]


def solve_kernel(cells, gram_ref, code_ref, out_ref, full, work):
    cases, lanes = out_ref.shape[1:3]
    case = lax.axis_index("case")
    block = 0
    for g in range(cases):
        for h in range(g, cases):
            value = gram_ref[block]
            full[g, h] = value
            if h != g:
                full[h, g] = value.T
            block += 1
    groups = [jnp.bitwise_xor(case, g) for g in range(cases)]
    grams = {(g, h): full[groups[g], groups[h]] for g in range(cases) for h in range(cases)}
    chains = [[0, 2 ** (LEVELS - 1)]]
    for level in range(LEVELS - 1, 0, -1):
        chains.insert(0, sorted({c ^ bit for c in chains[0] for bit in (0, 2**level)}))

    def joined(left, right):
        return jnp.concatenate([jnp.concatenate([grams[g, h] for h in right], 1) for g in left], 0)

    bases = {c: ([c], None) for c in range(cases)}
    for level in range(LEVELS):
        crossed = {}

        def cross(g, h):
            if (h, g) in crossed:
                return crossed[h, g].T
            if (g, h) not in crossed:
                value = dot(joined(bases[g][0], bases[h][0]), bases[h][1])
                crossed[g, h] = dot_rows(bases[g][1], value)
            return crossed[g, h]

        start = code_ref[level].astype(jnp.float32)
        coeffs, inners = [], []
        for c in chains[level]:
            pair = (c, c ^ 2**level)
            if level == 0:
                gram = joined(pair, pair)
            else:
                rows = []
                for g in pair:
                    parts = [cross(g, h) for h in pair]
                    rows.append(jnp.concatenate(parts, 1))
                gram = jnp.concatenate(rows, 0)
            first = dot(gram, start) / cells
            second = dot(gram, first) / cells
            coeff = second.astype(jnp.bfloat16).astype(jnp.float32)
            coeffs.append(coeff)
            inners.append(dot_rows(coeff, dot(gram, coeff)))
        inverses = inverse_factors(work, inners)
        updated = {}
        for i, c in enumerate(chains[level]):
            p = c ^ 2**level
            turned = lax.dot_general(
                coeffs[i], inverses[i], (((1,), (1,)), ((), ())), precision=HIGHEST, preferred_element_type=jnp.float32
            ) * math.sqrt(cells)
            if level == 0:
                updated[c] = ([c, p], turned)
            else:
                head, tail = turned[:lanes], turned[lanes:]
                updated[c] = (
                    bases[c][0] + bases[p][0],
                    jnp.concatenate([dot(bases[c][1], head), dot(bases[p][1], tail)], 0),
                )
        bases = updated
    for slot, c in enumerate(chains[-1]):
        members, matrix = bases[c]
        for i, g in enumerate(members):
            out_ref[slot, groups[g]] = matrix[i * lanes : (i + 1) * lanes].astype(out_ref.dtype)


def solve(cases, cells, grams, codes):
    lanes = grams.shape[-1]
    vmem = pl.BlockSpec(memory_space=pltpu.VMEM)
    return pl.pallas_call(
        functools.partial(solve_kernel, cells),
        out_shape=jax.ShapeDtypeStruct((2, cases, lanes, lanes), jnp.bfloat16),
        in_specs=[vmem] * 2,
        out_specs=vmem,
        scratch_shapes=[
            pltpu.VMEM((cases, cases, lanes, lanes), jnp.float32),
            pltpu.VMEM((cases, lanes, 2 * lanes), jnp.float32),
        ],
        compiler_params=pltpu.CompilerParams(vmem_limit_bytes=VMEM_BYTES),
    )(grams, codes)


def back_kernel(cases, s_ref, m_ref, out_ref, buffer, m_in, send, recv, m_send, m_recv):
    case, tile = lax.axis_index("case"), lax.axis_index("tile")
    core = lax.rem(tile, 2)
    cells = s_ref.shape[1]
    pieces = send.shape[1]
    chunk = cells // pieces
    beside = case + 1 - 2 * lax.rem(case, 2)
    devices = [{"case": lax.rem(case + cases // 2, cases)}, {"case": beside}, {"case": lax.rem(beside + cases // 2, cases)}]
    twin = {"tile": tile + 1 - 2 * core}
    sem = pltpu.get_barrier_semaphore()
    for device in devices + [twin]:
        pl.semaphore_signal(sem, inc=1, device_id=device, device_id_type=MESH)
    pl.semaphore_wait(sem, len(devices) + 1)

    depth = m_ref.shape[1] // 2
    part = pl.ds(pl.multiple_of(core * depth, depth), depth)
    across = remote(m_ref.at[:, part], m_in.at[:, part], m_send.at[0], m_recv.at[0], devices[1])
    swap = remote(m_in.at[:, part], m_in.at[:, part], m_send.at[1], m_recv.at[1], twin)
    across.start()

    def product(i, matrix):
        left = jnp.concatenate([s_ref[g, pl.ds(i * chunk, chunk), :] for g in range(cases)], 1)
        return jnp.dot(left, matrix, preferred_element_type=jnp.float32).astype(out_ref.dtype)

    copies = []

    def deliver(i, k, matrix):
        at = pl.ds(i * chunk, chunk)
        buffer[k, at, :] = product(i, matrix)
        copy = remote(buffer.at[k, at], out_ref.at[case, at], send.at[k, i], recv.at[k, i], devices[k])
        copy.start()
        copies.append(copy)

    for i in range(pieces):
        deliver(i, 0, m_ref[1])
    across.wait()
    swap.start()
    for i in range(pieces):
        out_ref[case, pl.ds(i * chunk, chunk), :] = product(i, m_ref[0])
    swap.wait()
    for i in range(pieces):
        for k in (1, 2):
            deliver(i, k, m_in[k - 1])
    for copy in copies:
        copy.wait()


def back(cases, snaps, matrices):
    vmem = pl.BlockSpec(memory_space=pltpu.VMEM)
    return pl.pallas_call(
        functools.partial(back_kernel, cases),
        out_shape=jax.ShapeDtypeStruct(snaps.shape, jnp.bfloat16),
        in_specs=[vmem] * 2,
        out_specs=vmem,
        scratch_shapes=[
            pltpu.VMEM(snaps.shape, jnp.bfloat16),
            pltpu.VMEM(matrices.shape, jnp.bfloat16),
            pltpu.SemaphoreType.DMA((cases, 4)),
            pltpu.SemaphoreType.DMA((cases, 4)),
            pltpu.SemaphoreType.DMA((2,)),
            pltpu.SemaphoreType.DMA((2,)),
        ],
        compiler_params=pltpu.CompilerParams(collective_id=1, has_side_effects=True, vmem_limit_bytes=VMEM_BYTES),
    )(snaps, matrices)


def per_device(cases, tiles, forcing, permeability, merge_weights, start_codes):
    _, rows, ny, lanes = forcing.shape
    snaps, grams = front(cases, tiles, forcing[0], permeability[0], merge_weights)
    cells = rows * tiles * ny
    matrices = solve(cases, cells, grams.reshape(-1, lanes, lanes), start_codes)
    basis = back(cases, snaps.reshape(cases, -1, lanes), matrices.reshape(2, -1, lanes))
    return basis.reshape(1, -1, lanes)


def solution(mesh):
    placed = (P("case", "tile", None, None), P("case", "tile", None), P("case"), P())
    return jax.shard_map(
        functools.partial(per_device, mesh.shape["case"], mesh.shape["tile"]),
        mesh=mesh, in_specs=placed, out_specs=P("case", "tile", None), check_vma=False,
    )
```

```python
import functools
import math

import jax
import jax.numpy as jnp
from jax import lax
from jax.experimental import pallas as pl
from jax.experimental.pallas import tpu as pltpu
from jax.sharding import PartitionSpec as P

STEPS = 3
LEVELS = 2
PAD = 8
PANEL = 32
GROUP = 16
HIGHEST = lax.Precision.HIGHEST
MESH = pl.DeviceIdType.MESH
VMEM_BYTES = 60 * 2**20


def peers(axis, size):
    me = lax.axis_index(axis)
    return [{axis: lax.rem(me + k, size)} for k in range(size)]


def barrier(*axes):
    sem = pltpu.get_barrier_semaphore()
    count = 0
    for axis, size in axes:
        for device in peers(axis, size)[1:]:
            pl.semaphore_signal(sem, inc=1, device_id=device, device_id_type=MESH)
            count += 1
    pl.semaphore_wait(sem, count)


def remote(src, dst, send, recv, device):
    return pltpu.make_async_remote_copy(
        src_ref=src, dst_ref=dst, send_sem=send, recv_sem=recv, device_id=device, device_id_type=MESH
    )


def front_kernel(
    cases, tiles, f_ref, p_ref, weight_ref, s_ref, gram_ref,
    halo, p_ext, p_turned, u, wide_a, wide_b, out, flat, part, core_in, core_sum, case_in, acc, chip_in,
    halo_send, halo_recv, p_send, p_recv, s_send, s_recv,
    rs_send, rs_recv, cs_send, cs_recv, ts_send, ts_recv, tg_send, tg_recv, cg_send, cg_recv, rg_send, rg_recv,
):
    rows, ny, lanes = f_ref.shape
    ext = rows + 2 * STEPS
    quarter = rows // cases
    case, tile = lax.axis_index("case"), lax.axis_index("tile")
    case_peers, tile_peers = peers("case", cases), peers("tile", tiles)
    chunk = 128
    barrier(("case", cases), ("tile", tiles))

    back = remote(f_ref.at[pl.ds(0, STEPS)], halo.at[1], halo_send.at[0], halo_recv.at[1], {"tile": tile - 1})
    ahead = remote(f_ref.at[pl.ds(rows - STEPS, STEPS)], halo.at[0], halo_send.at[1], halo_recv.at[0], {"tile": tile + 1})

    p_back = remote(
        p_ref.at[pl.ds(0, PAD)], p_ext.at[pl.ds(PAD + rows, PAD)], p_send.at[0], p_recv.at[1], {"tile": tile - 1}
    )
    p_ahead = remote(
        p_ref.at[pl.ds(rows - PAD, PAD)], p_ext.at[pl.ds(0, PAD)], p_send.at[1], p_recv.at[0], {"tile": tile + 1}
    )

    @pl.when(tile > 0)
    def _():
        p_back.start()
        back.start()

    @pl.when(tile < tiles - 1)
    def _():
        p_ahead.start()
        ahead.start()

    @pl.when(tile == 0)
    def _():
        p_ext[0:PAD] = jnp.zeros((PAD, ny), jnp.float32)

    @pl.when(tile == tiles - 1)
    def _():
        p_ext[PAD + rows : 2 * PAD + rows] = jnp.zeros((PAD, ny), jnp.float32)

    p_ext[PAD : PAD + rows] = p_ref[...]
    p_ext[2 * PAD + rows :] = jnp.zeros((lanes - 2 * PAD - rows, ny), jnp.float32)
    p_turned[0:PAD] = jnp.zeros((PAD, lanes), jnp.float32)
    p_turned[PAD + ny :] = jnp.zeros((PAD, lanes), jnp.float32)

    @pl.loop(0, ext)
    def _(r):
        zeros = jnp.zeros((PAD, lanes), jnp.float32)
        for at in (pl.ds(0, PAD), pl.ds(PAD + ny, PAD)):
            wide_a[r, at] = zeros
            for slot in range(STEPS):
                u[slot, r, at] = zeros

    @pl.when(tile > 0)
    def _():
        p_back.wait_send()
        p_ahead.wait_recv()

    @pl.when(tile < tiles - 1)
    def _():
        p_ahead.wait_send()
        p_back.wait_recv()

    for y in range(0, ny, lanes):
        p_turned[pl.ds(PAD + y, lanes)] = p_ext[:, y : y + lanes].T
    for y in range(0, ny, 64):
        mid = p_turned[pl.ds(PAD + y, 64)]
        around = p_turned[pl.ds(PAD + y + 1, 64)] + p_turned[pl.ds(PAD + y - 1, 64)]
        around = around + (pltpu.roll(mid, 1, 1) + pltpu.roll(mid, lanes - 1, 1))
        col_a = 0.12 * mid
        col_b = 1.0 - 0.12 * (4.0 * mid + around)
        for r in range(ext):
            at = r + PAD - STEPS
            wide_a[r, pl.ds(PAD + y, 64)] = jnp.broadcast_to(col_a[:, at : at + 1], (64, lanes))
            wide_b[r, pl.ds(y, 64)] = jnp.broadcast_to(col_b[:, at : at + 1], (64, lanes))

    def take(r, load):
        for y in range(0, ny, chunk):
            u[0, r, pl.ds(PAD + y, chunk)] = load(y).astype(jnp.float32)

    @pl.loop(0, rows)
    def _(r):
        take(r + STEPS, lambda y: f_ref[r, pl.ds(y, chunk)])

    @pl.when(tile > 0)
    def _():
        back.wait_send()
        ahead.wait_recv()

    @pl.when(tile < tiles - 1)
    def _():
        ahead.wait_send()
        back.wait_recv()

    @pl.when(tile == 0)
    def _():
        halo[0] = jnp.zeros((STEPS, ny, lanes), halo.dtype)

    @pl.when(tile == tiles - 1)
    def _():
        halo[1] = jnp.zeros((STEPS, ny, lanes), halo.dtype)

    @pl.loop(0, STEPS)
    def _(r):
        take(r, lambda y: halo[0, r, pl.ds(y, chunk)])
        take(r + STEPS + rows, lambda y: halo[1, r, pl.ds(y, chunk)])

    def stepped(src, r, y):
        at = pl.ds(PAD + y, chunk)
        sides = (r + 1, at), (r - 1, at), (r, pl.ds(PAD + y + 1, chunk)), (r, pl.ds(PAD + y - 1, chunk))
        coef = wide_a[r, at]
        value = wide_b[r, pl.ds(y, chunk)] * u[src, r, at]
        for i, j in sides:
            value = value + (coef + wide_a[i, j]) * u[src, i, j]
        return value

    def advance(step, low, high):
        def one(r, _):
            inside = ((r >= STEPS) | (tile > 0)) & ((r < STEPS + rows) | (tile < tiles - 1))
            mask = jnp.where(inside, 1.0, 0.0)
            for y in range(0, ny, chunk):
                u[step + 1, r, pl.ds(PAD + y, chunk)] = stepped(step, r, y) * mask
            return 0

        lax.fori_loop(low, high, one, 0)

    weight = jnp.sqrt(jnp.full((1, lanes), weight_ref[0].astype(jnp.float32)))
    def row_copy(k, i):
        return remote(out.at[k, i], s_ref.at[case, i], s_send.at[k, i], s_recv.at[k, i], case_peers[k])

    for k in [k for k in range(cases) if k] + [0]:
        turn = lax.rem(case + k, cases)
        first = turn * quarter
        for step in range(STEPS - 1):
            reach = STEPS - 1 - step
            low = -reach if k == 1 else jnp.where(turn == 0, -reach, reach)
            advance(step, first + STEPS + low, first + STEPS + quarter + reach)

        @pl.loop(0, quarter)
        def _(i):
            for y in range(0, ny, chunk):
                value = (stepped(STEPS - 1, first + i + STEPS, y) * weight).astype(jnp.bfloat16)
                if k:
                    out[k, i, pl.ds(y, chunk)] = value
                else:
                    s_ref[case, i, pl.ds(y, chunk)] = value

            if k:
                row_copy(k, i).start()

    for i in range(quarter):
        for k in range(1, cases):
            row_copy(k, i).wait()

    block = 0
    snaps = [s_ref[g].reshape(quarter * ny, lanes) for g in range(cases)]
    for g in range(cases):
        right = jnp.concatenate(snaps[g:], 1)
        terms = lax.dot_general(snaps[g], right, (((0,), (0,)), ((), ())), preferred_element_type=jnp.float32)
        for h in range(cases - g):
            flat[block * lanes : (block + 1) * lanes, :] = terms[:, h * lanes : (h + 1) * lanes]
            block += 1
    half, share = part.shape[2:4]
    for i in range(2 * cases * half):
        part[i // (cases * half), i // half % cases, i % half] = flat[i * share : (i + 1) * share, :]

    def exchange(devices, source, target, send, recv):
        started = [remote(source(k), target(k), send.at[k], recv.at[k], devices[k]) for k in range(1, len(devices))]
        for copy in started:
            copy.start()
        for copy in started:
            copy.wait()

    core, chip = lax.rem(tile, 2), lax.div(tile, 2)
    core_peers = [{"tile": tile}, {"tile": chip * 2 + 1 - core}]
    chip_peers = [{"tile": lax.rem(chip + k, half) * 2 + core} for k in range(half)]
    exchange(core_peers, lambda k: part.at[1 - core], lambda k: core_in, rs_send, rs_recv)
    core_sum[...] = part[core] + core_in[...]
    exchange(
        case_peers, lambda k: core_sum.at[lax.rem(case + k, cases)], lambda k: case_in.at[k], cs_send, cs_recv
    )
    total = core_sum[case]
    for k in range(1, cases):
        total = total + case_in[k]
    acc[...] = total
    exchange(
        chip_peers, lambda k: acc.at[lax.rem(chip + k, half)], lambda k: chip_in.at[k], ts_send, ts_recv
    )
    total = acc[chip]
    for k in range(1, half):
        total = total + chip_in[k]
    gram_ref[core, case, chip] = total
    mine = gram_ref.at[core, case, chip]
    exchange(chip_peers, lambda k: mine, lambda k: mine, tg_send, tg_recv)
    ours = gram_ref.at[core, case]
    exchange(case_peers, lambda k: ours, lambda k: ours, cg_send, cg_recv)
    exchange(core_peers, lambda k: gram_ref.at[core], lambda k: gram_ref.at[core], rg_send, rg_recv)


def front(cases, tiles, forcing, permeability, merge_weights):
    rows, ny, lanes = forcing.shape
    ext, quarter = rows + 2 * STEPS, rows // cases
    total = cases * (cases + 1) // 2 * lanes
    half = tiles // 2
    share = total // (2 * cases * half)
    f32, bf16 = jnp.float32, jnp.bfloat16
    vmem = pl.BlockSpec(memory_space=pltpu.VMEM)
    dma = pltpu.SemaphoreType.DMA
    return pl.pallas_call(
        functools.partial(front_kernel, cases, tiles),
        out_shape=(
            jax.ShapeDtypeStruct((cases, quarter, ny, lanes), bf16),
            jax.ShapeDtypeStruct((2, cases, half, share, lanes), f32),
        ),
        in_specs=[vmem, vmem, pl.BlockSpec(memory_space=pltpu.SMEM)],
        out_specs=(vmem, vmem),
        scratch_shapes=[
            pltpu.VMEM((2, STEPS, ny, lanes), bf16),
            pltpu.VMEM((lanes, ny), f32),
            pltpu.VMEM((ny + 2 * PAD, lanes), f32),
            pltpu.VMEM((STEPS, ext, ny + 2 * PAD, lanes), f32),
            pltpu.VMEM((ext, ny + 2 * PAD, lanes), f32),
            pltpu.VMEM((ext, ny, lanes), f32),
            pltpu.VMEM((cases, quarter, ny, lanes), bf16),
            pltpu.VMEM((total, lanes), f32),
            pltpu.VMEM((2, cases, half, share, lanes), f32),
            pltpu.VMEM((cases, half, share, lanes), f32),
            pltpu.VMEM((cases, half, share, lanes), f32),
            pltpu.VMEM((cases, half, share, lanes), f32),
            pltpu.VMEM((half, share, lanes), f32),
            pltpu.VMEM((half, share, lanes), f32),
            dma((2,)), dma((2,)),
            dma((2,)), dma((2,)),
            dma((cases, quarter)), dma((cases, quarter)),
            dma((2,)), dma((2,)),
            dma((cases,)), dma((cases,)),
            dma((half,)), dma((half,)),
            dma((half,)), dma((half,)),
            dma((cases,)), dma((cases,)),
            dma((2,)), dma((2,)),
        ],
        compiler_params=pltpu.CompilerParams(collective_id=0, has_side_effects=True, vmem_limit_bytes=VMEM_BYTES),
    )(forcing, permeability, merge_weights)


def dot(left, right):
    return jnp.dot(left, right, precision=HIGHEST, preferred_element_type=jnp.float32)


def dot_rows(left, right):
    return lax.dot_general(
        left, right, (((0,), (0,)), ((), ())), precision=HIGHEST, preferred_element_type=jnp.float32
    )


def inverse_factors(work, inners):
    count, size = len(inners), inners[0].shape[0]
    eye = (
        lax.broadcasted_iota(jnp.int32, (size, size), 0) == lax.broadcasted_iota(jnp.int32, (size, size), 1)
    ).astype(jnp.float32)
    for b in range(count):
        work[b, :, :size] = inners[b]
        work[b, :, size:] = eye
    shape = (count, PANEL, size)
    index = lax.broadcasted_iota(jnp.int32, shape, 1)
    for top in range(0, size, PANEL):
        left = work[:count, top : top + PANEL, :size]
        right = work[:count, top : top + PANEL, size:]
        scale = jnp.ones(shape, jnp.float32)
        for group in range(0, PANEL, GROUP):
            at = top + group
            columns = [jnp.broadcast_to(left[:, :, at + j : at + j + 1], shape) for j in range(GROUP)]
            for j in range(GROUP):
                i = group + j
                root = lax.rsqrt(columns[j][:, i : i + 1, :])
                scale = jnp.where(index == i, root, scale)
                factor = jnp.where(index > i, columns[j] * (root * root), 0.0)
                for m in range(j + 1, GROUP):
                    columns[m] = columns[m] - factor * columns[m][:, i : i + 1, :]
                left = left - factor * left[:, i : i + 1, :]
                right = right - factor * right[:, i : i + 1, :]
        panel = jnp.concatenate([left * scale, right * scale], 2)
        work[:count, top : top + PANEL, :] = panel
        below = top + PANEL
        if below < size:
            for b in range(count):
                lead = panel[b][:, :size]
                update = dot_rows(lead, panel[b])
                work[b, below:, :] = work[b, below:, :] - update[below:, :]
    return [work[b, :, size:] for b in range(count)]


def solve_kernel(cells, gram_ref, code_ref, out_ref, full, work):
    cases, lanes = out_ref.shape[1:3]
    case = lax.axis_index("case")
    block = 0
    for g in range(cases):
        for h in range(g, cases):
            value = gram_ref[block]
            full[g, h] = value
            if h != g:
                full[h, g] = value.T
            block += 1
    groups = [jnp.bitwise_xor(case, g) for g in range(cases)]
    grams = {(g, h): full[groups[g], groups[h]] for g in range(cases) for h in range(cases)}
    chains = [[0, 2 ** (LEVELS - 1)]]
    for level in range(LEVELS - 1, 0, -1):
        chains.insert(0, sorted({c ^ bit for c in chains[0] for bit in (0, 2**level)}))

    def joined(left, right):
        return jnp.concatenate([jnp.concatenate([grams[g, h] for h in right], 1) for g in left], 0)

    bases = {c: ([c], None) for c in range(cases)}
    for level in range(LEVELS):
        crossed = {}

        def cross(g, h):
            if (h, g) in crossed:
                return crossed[h, g].T
            if (g, h) not in crossed:
                value = dot(joined(bases[g][0], bases[h][0]), bases[h][1])
                crossed[g, h] = dot_rows(bases[g][1], value)
            return crossed[g, h]

        start = code_ref[level].astype(jnp.float32)
        coeffs, inners = [], []
        for c in chains[level]:
            pair = (c, c ^ 2**level)
            if level == 0:
                gram = joined(pair, pair)
            else:
                rows = []
                for g in pair:
                    parts = [cross(g, h) for h in pair]
                    rows.append(jnp.concatenate(parts, 1))
                gram = jnp.concatenate(rows, 0)
            first = dot(gram, start) / cells
            second = dot(gram, first) / cells
            coeff = second.astype(jnp.bfloat16).astype(jnp.float32)
            coeffs.append(coeff)
            inners.append(dot_rows(coeff, dot(gram, coeff)))
        inverses = inverse_factors(work, inners)
        updated = {}
        for i, c in enumerate(chains[level]):
            p = c ^ 2**level
            turned = lax.dot_general(
                coeffs[i], inverses[i], (((1,), (1,)), ((), ())), precision=HIGHEST, preferred_element_type=jnp.float32
            ) * math.sqrt(cells)
            if level == 0:
                updated[c] = ([c, p], turned)
            else:
                head, tail = turned[:lanes], turned[lanes:]
                updated[c] = (
                    bases[c][0] + bases[p][0],
                    jnp.concatenate([dot(bases[c][1], head), dot(bases[p][1], tail)], 0),
                )
        bases = updated
    for slot, c in enumerate(chains[-1]):
        members, matrix = bases[c]
        for i, g in enumerate(members):
            out_ref[slot, groups[g]] = matrix[i * lanes : (i + 1) * lanes].astype(out_ref.dtype)


def solve(cases, cells, grams, codes):
    lanes = grams.shape[-1]
    vmem = pl.BlockSpec(memory_space=pltpu.VMEM)
    return pl.pallas_call(
        functools.partial(solve_kernel, cells),
        out_shape=jax.ShapeDtypeStruct((2, cases, lanes, lanes), jnp.bfloat16),
        in_specs=[vmem] * 2,
        out_specs=vmem,
        scratch_shapes=[
            pltpu.VMEM((cases, cases, lanes, lanes), jnp.float32),
            pltpu.VMEM((cases, lanes, 2 * lanes), jnp.float32),
        ],
        compiler_params=pltpu.CompilerParams(vmem_limit_bytes=VMEM_BYTES),
    )(grams, codes)


def back_kernel(cases, s_ref, m_ref, out_ref, buffer, m_in, send, recv, m_send, m_recv):
    case, tile = lax.axis_index("case"), lax.axis_index("tile")
    core = lax.rem(tile, 2)
    cells = s_ref.shape[1]
    pieces = send.shape[1]
    chunk = cells // pieces
    beside = case + 1 - 2 * lax.rem(case, 2)
    devices = [{"case": lax.rem(case + cases // 2, cases)}, {"case": beside}, {"case": lax.rem(beside + cases // 2, cases)}]
    twin = {"tile": tile + 1 - 2 * core}
    sem = pltpu.get_barrier_semaphore()
    for device in devices + [twin]:
        pl.semaphore_signal(sem, inc=1, device_id=device, device_id_type=MESH)
    pl.semaphore_wait(sem, len(devices) + 1)

    depth = m_ref.shape[1] // 2
    part = pl.ds(pl.multiple_of(core * depth, depth), depth)
    across = remote(m_ref.at[:, part], m_in.at[:, part], m_send.at[0], m_recv.at[0], devices[1])
    swap = remote(m_in.at[:, part], m_in.at[:, part], m_send.at[1], m_recv.at[1], twin)
    across.start()

    def product(i, matrix):
        left = jnp.concatenate([s_ref[g, pl.ds(i * chunk, chunk), :] for g in range(cases)], 1)
        return jnp.dot(left, matrix, preferred_element_type=jnp.float32).astype(out_ref.dtype)

    copies = []

    def deliver(i, k, matrix):
        at = pl.ds(i * chunk, chunk)
        buffer[k, at, :] = product(i, matrix)
        copy = remote(buffer.at[k, at], out_ref.at[case, at], send.at[k, i], recv.at[k, i], devices[k])
        copy.start()
        copies.append(copy)

    for i in range(pieces):
        deliver(i, 0, m_ref[1])
    across.wait()
    swap.start()
    for i in range(pieces):
        out_ref[case, pl.ds(i * chunk, chunk), :] = product(i, m_ref[0])
    swap.wait()
    for i in range(pieces):
        for k in (1, 2):
            deliver(i, k, m_in[k - 1])
    for copy in copies:
        copy.wait()


def back(cases, snaps, matrices):
    vmem = pl.BlockSpec(memory_space=pltpu.VMEM)
    return pl.pallas_call(
        functools.partial(back_kernel, cases),
        out_shape=jax.ShapeDtypeStruct(snaps.shape, jnp.bfloat16),
        in_specs=[vmem] * 2,
        out_specs=vmem,
        scratch_shapes=[
            pltpu.VMEM(snaps.shape, jnp.bfloat16),
            pltpu.VMEM(matrices.shape, jnp.bfloat16),
            pltpu.SemaphoreType.DMA((cases, 4)),
            pltpu.SemaphoreType.DMA((cases, 4)),
            pltpu.SemaphoreType.DMA((2,)),
            pltpu.SemaphoreType.DMA((2,)),
        ],
        compiler_params=pltpu.CompilerParams(collective_id=1, has_side_effects=True, vmem_limit_bytes=VMEM_BYTES),
    )(snaps, matrices)


def per_device(cases, tiles, forcing, permeability, merge_weights, start_codes):
    _, rows, ny, lanes = forcing.shape
    snaps, grams = front(cases, tiles, forcing[0], permeability[0], merge_weights)
    cells = rows * tiles * ny
    matrices = solve(cases, cells, grams.reshape(-1, lanes, lanes), start_codes)
    basis = back(cases, snaps.reshape(cases, -1, lanes), matrices.reshape(2, -1, lanes))
    return basis.reshape(1, -1, lanes)


def solution(mesh):
    placed = (P("case", "tile", None, None), P("case", "tile", None), P("case"), P())
    return jax.shard_map(
        functools.partial(per_device, mesh.shape["case"], mesh.shape["tile"]),
        mesh=mesh, in_specs=placed, out_specs=P("case", "tile", None), check_vma=False,
    )
```
